512 devices in a mesh: dp: 64 (over x, z), mp: 8 (over y, core).
Axes of the slice: x: 4, y: 4, z: 16, core: 2. Of those that a mesh axis runs over, the one named last changes fastest.
Arguments:
- value_grads: bfloat16 [73728, 1024], P('dp', 'mp'), may hold values from -90 to 90
- activations: bfloat16 [73728, 5120], P(('dp', 'mp')), may hold values from -90 to 90
- block_moment: float32 [1032], replicated, may hold values from 368640 to 36864000
- first_moment: float32 [8, 5184, 128], P('mp', 'dp'), may hold values from -32768 to 32768
Outputs:
- update: float32 [8, 5184, 128], P('mp', 'dp')
The draws below stay inside these ranges and needn't reach their ends.
All inputs are finite; a program needn't handle non-finite values.
Results may differ from the reference program's by a relative error of at most 0.0003.
Values may be sent and summed in bfloat16 or wider, within the bound.
A program may use at most 64 MiB of HBM per device.

```python
import math
import jax
import jax.numpy as jnp
from jax import lax

D = 5120
HEAD_DIM = 128
KV_HEADS = 8
VALUE_UNITS = 1024
TOKENS = 73728
USED = 655488
FLAT_ROWS = 5184


def scaled_field(values, key_cols, row_count, col_count, top):
    col_scale = jnp.exp(jax.random.uniform(key_cols, (1, col_count), jnp.float32) * jnp.log(top))
    row_pos = jnp.arange(row_count, dtype=jnp.float32)[:, None]
    col_pos = jnp.arange(col_count, dtype=jnp.float32)[None, :]
    rising = (1.0 + 2.0 * row_pos / (row_count - 1)) * (1.0 + 2.0 * col_pos / (col_count - 1))
    return values * col_scale * rising * 0.25


def draw_value_grads(key, part):
    key = jax.random.fold_in(key, 17)
    key_vals, key_cols = jax.random.split(key)
    values = jnp.clip(jax.random.normal(key_vals, (TOKENS, VALUE_UNITS), jnp.float32), -4.0, 4.0)
    top = 10.0
    return scaled_field(values, key_cols, TOKENS, VALUE_UNITS, top).astype(jnp.bfloat16)


def draw_activations(key, part):
    key = jax.random.fold_in(key, 29)
    key_vals, key_cols = jax.random.split(key)
    values = jnp.clip(jax.random.normal(key_vals, (TOKENS, D), jnp.float32), -4.0, 4.0)
    top = 10.0
    return scaled_field(values, key_cols, TOKENS, D, top).astype(jnp.bfloat16)


def levels(stream_key, dims, pieces, least, high):
    factor_of, own = 1.0, jax.random.fold_in(stream_key, 6)
    for axis_at, shards_of in pieces:
        heights = jnp.exp(jax.random.uniform(jax.random.fold_in(own, axis_at), (shards_of,), jnp.float32, least / len(pieces), high / len(pieces)))
        factor_of = factor_of * jnp.repeat(heights, dims[axis_at] // shards_of).reshape([-1 if axis == axis_at else 1 for axis in range(len(dims))])
    return factor_of


def scatter_about(key, dims, deviation, bound, cuts=(), kind=jnp.bfloat16):
    level = levels(key, dims, cuts, -0.22, 0.18) if cuts else 1.0
    values = jax.random.normal(key, dims, jnp.float32) * deviation * level
    return jnp.minimum(jnp.maximum(values, -bound), bound).astype(kind)


def setup_inputs(seed: int = 0) -> dict:
    streams_of = jax.random.split(jax.random.key(seed), 5)
    value_grads = draw_value_grads(jax.random.fold_in(streams_of[4], 71), 0)
    activations = draw_activations(jax.random.fold_in(streams_of[4], 71), 0)
    block_moment = jnp.clip(jnp.exp(jax.random.uniform(streams_of[2], (VALUE_UNITS + KV_HEADS,), jnp.float32, math.log(368640.0), math.log(36864000))), 368640.0, 36864000)
    first_moment = scatter_about(streams_of[3], (KV_HEADS, FLAT_ROWS, 128), (20 * TOKENS ** 0.5), 32768.0, ((0, 8), (1, 64)), jnp.float32)
    return {"value_grads": value_grads, "activations": activations, "block_moment": block_moment, "first_moment": first_moment}


beta_one = 0.9
beta_two = 0.95
bias_one = 1.0 - 0.9 ** 10
bias_two = 1.0 - 0.95 ** 10
epsilon = 1e-08

def reference(value_grads, activations, block_moment, first_moment):
    weight_grad = jnp.dot(value_grads.T, activations, preferred_element_type=jnp.float32)
    bias_grad = lax.optimization_barrier(jnp.sum(value_grads.astype(jnp.float32), axis=0))
    unit_total = lax.optimization_barrier(jnp.sum(weight_grad * weight_grad, axis=1))
    unit_moment = beta_two * block_moment[:VALUE_UNITS] + (1.0 - beta_two) * (unit_total / D)
    position = jnp.arange(FLAT_ROWS * 128, dtype=jnp.int32)
    unit_of = jnp.clip((position - HEAD_DIM) // D, 0, HEAD_DIM - 1).astype(jnp.int32)
    updates = []
    for head in range(KV_HEADS):
        head_bias = bias_grad[head * HEAD_DIM:(head + 1) * HEAD_DIM]
        head_total = jnp.sum(head_bias * head_bias)
        head_moment = beta_two * block_moment[VALUE_UNITS + head] + (1.0 - beta_two) * (head_total / HEAD_DIM)
        padding = jnp.zeros((FLAT_ROWS * 128 - USED,), jnp.float32)
        flat = jnp.concatenate([head_bias, weight_grad[head * HEAD_DIM:(head + 1) * HEAD_DIM, :].reshape(-1), padding])
        head_units = unit_moment[head * HEAD_DIM:(head + 1) * HEAD_DIM]
        moment_field = jnp.where(position < HEAD_DIM, head_moment, jnp.where(position < USED, head_units[unit_of], 0.0))
        momentum = beta_one * first_moment[head].reshape(-1) + (1.0 - beta_one) * flat
        step_dir = jnp.where(position < USED, momentum / bias_one / (jnp.sqrt(moment_field / bias_two) + epsilon), 0.0)
        updates.append(step_dir.reshape(FLAT_ROWS, 128))
    return jnp.stack(updates)
```

```python
import functools

import jax
import jax.numpy as jnp
import numpy as np
from jax import lax
from jax.experimental import pallas as pl
from jax.experimental.pallas import tpu as pltpu
from jax.sharding import PartitionSpec as P

MESH = pl.DeviceIdType.MESH

beta_one = 0.9
beta_two = 0.95
bias_one = 1.0 - 0.9**10
bias_two = 1.0 - 0.95**10
epsilon = 1e-08

NX, NZ, NY, NC = 4, 16, 4, 2
NDP, NMP = NX * NZ, NY * NC
LANES = 128
HEAD = 128
TOK = 144
TOKENS = TOK * NMP
WIDTH = 5120
SLICE = WIDTH // NMP
CH = SLICE // LANES
ROWS_P = 81
USED_ROWS = 1 + HEAD * WIDTH // LANES
UNIT_ROWS = WIDTH // LANES


def unit_order():
    order = np.zeros((HEAD, HEAD), np.float32)
    for e in range(2):
        for x in range(NX):
            for zl in range(4):
                for zh in range(4):
                    q = x * 16 + zl * 4 + zh
                    p = x * 16 + zh * 4 + zl
                    order[e * 64 + q, 2 * p + e] = 1.0
    return order


def kernel(
    perm_ref, vg_ref, act_ref, block_ref, first_ref, out_ref,
    vt, a_buf, r_buf, x1, s1, x2, near_out, near_in, far_out, far_in, g_buf, g_in, rows, denom,
    bias_out, bias_x, bias_n, bias_f,
    v_send, v_recv, w_send, a_send, a_recv, x1_send, x1_recv, x2_send, x2_recv,
    n_send, n_recv, f_send, f_recv, g_send, g_recv, b_send, b_recv,
):
    dp, mp = lax.axis_index("dp"), lax.axis_index("mp")
    x, z = dp // NZ, dp % NZ
    zh, zl = z // 4, z % 4
    y, c = mp // NC, mp % NC

    def at(px=None, pz=None, m=None, p=None):
        if p is None:
            p = (x if px is None else px) * NZ + (z if pz is None else pz)
        return {"dp": p, "mp": mp if m is None else m}

    def remote(src, dst, send, recv, device):
        return pltpu.make_async_remote_copy(
            src_ref=src, dst_ref=dst, send_sem=send, recv_sem=recv, device_id=device, device_id_type=MESH
        )

    mp_others = [(mp + k) % NMP for k in range(1, NMP)]
    y_others = [(y + k) % NY for k in range(1, NY)]
    x_others = [(x + k) % NX for k in range(1, NX)]
    zl_others = [(zl + k) % 4 for k in range(1, 4)]
    zh_others = [(zh + k) % 4 for k in range(1, 4)]
    before, after = (dp + NDP - 1) % NDP, (dp + 1) % NDP
    odd = x % 2
    pair = x + 1 - 2 * odd
    cross = (x + NX - 1 + 2 * odd) % NX

    def cross_of(v):
        return (v + NX - 1 + 2 * (v % 2)) % NX

    def pair_of(v):
        return v + 1 - 2 * (v % 2)

    with jax.named_scope("entry"):
        barrier = pltpu.get_barrier_semaphore()
        partners = [at(m=m) for m in mp_others]
        partners += [at(px=v) for v in x_others]
        partners += [at(pz=zh * 4 + v) for v in zl_others]
        partners += [at(pz=v * 4 + zl) for v in zh_others]
        partners += [at(p=p, m=m) for p in (before, after) for m in range(NMP)]
        for partner in partners:
            pl.semaphore_signal(barrier, inc=1, device_id=partner, device_id_type=MESH)
        for j in range(CH):
            columns = pl.ds(pl.multiple_of(mp * SLICE + j * LANES, LANES), LANES)
            own = pl.ds(pl.multiple_of(mp * TOK, TOK), TOK)
            pltpu.make_async_copy(act_ref.at[:, columns], a_buf.at[j, own], a_recv.at[j]).start()
    with jax.named_scope("turn"):
        vt[mp] = lax.dot_general(
            perm_ref[...], vg_ref[...], (((1,), (1,)), ((), ())), preferred_element_type=jnp.float32
        ).astype(jnp.bfloat16)
        bias = jnp.sum(vg_ref[...].astype(jnp.float32), axis=0, keepdims=True)
        bias_out[0] = jnp.broadcast_to(bias, (8, LANES))
    with jax.named_scope("barrier"):
        pl.semaphore_wait(barrier, len(partners))

    def v_copy(v, slot):
        return remote(vt.at[slot], vt.at[slot], v_send, v_recv.at[slot], at(m=v * NC + c))

    def w_copy(slot):
        return remote(vt.at[slot], vt.at[slot], w_send, v_recv.at[slot], at(m=y * NC + 1 - c))

    def a_copy(j, m):
        columns = pl.ds(pl.multiple_of(m * SLICE + j * LANES, LANES), LANES)
        own = pl.ds(pl.multiple_of(mp * TOK, TOK), TOK)
        return remote(act_ref.at[:, columns], a_buf.at[j, own], a_send.at[j], a_recv.at[j], at(m=m))

    with jax.named_scope("send"):
        for v in y_others:
            v_copy(v, mp).start()
        w_copy(mp).start()
        for j in range(CH):
            for m in mp_others:
                a_copy(j, m).start()

        @pl.when(x != 0)
        def _():
            remote(bias_out.at[0], bias_x.at[x], b_send.at[0], b_recv.at[0], at(px=0)).start()

    with jax.named_scope("forward"):
        for v in y_others:
            slot = v * NC + c
            v_copy(y, slot).wait_recv()
            w_copy(slot).start()
        for v in range(NY):
            w_copy(v * NC + 1 - c).wait_recv()

    def first_of(half):
        return (pair, cross_of(pair)) if half == 0 else (cross, pair_of(cross))

    def second_of(half):
        return cross if half == 0 else pair

    def block(b):
        return pl.ds(pl.multiple_of(b * 128, 128), 128)

    def x1_copies(j, half):
        to, other = first_of(half)
        return [
            remote(r_buf.at[j, half, block(b)], x1.at[j, half, k], x1_send.at[j, half], x1_recv.at[j, half, k], at(px=to))
            for k, b in ((1, other), (0, to))
        ]

    def x2_copy(j, half):
        return remote(s1.at[j, half], x2.at[j, half], x2_send.at[j, half], x2_recv.at[j, half], at(px=second_of(half)))

    def near_copy(j, v):
        return remote(near_out.at[j, v], near_in.at[j, zl], n_send.at[j], n_recv.at[j], at(pz=zh * 4 + v))

    def far_copy(j, v):
        return remote(far_out.at[j, v], far_in.at[j, zh], f_send.at[j], f_recv.at[j], at(pz=v * 4 + zl))

    def stage_mul(j):
        with jax.named_scope("mul"):
            pltpu.make_async_copy(a_buf.at[j], a_buf.at[j], a_recv.at[j]).wait()
            for half in range(2):
                for v in range(NY):
                    res = jnp.dot(vt[v * NC + half], a_buf[j], preferred_element_type=jnp.float32)
                    for e in range(2):
                        r_buf[j, half, pl.ds(v * 2 + e, 64, stride=8), :] = res[e * 64 : (e + 1) * 64]
                for copy in x1_copies(j, half):
                    copy.start()

    def stage_x1(j):
        with jax.named_scope("x1"):
            for half in range(2):
                copies = x1_copies(j, half)
                copies[0].wait_recv()
                s1[j, half] = r_buf[j, half, block(second_of(half))] + x1[j, half, 1]
                x2_copy(j, half).start()
            for half in range(2):
                x1_copies(j, half)[1].wait_recv()

    def stage_x2(j):
        with jax.named_scope("x2"):
            for half in range(2):
                x2_copy(j, half).wait_recv()
                total = r_buf[j, half, block(x)] + x1[j, half, 0] + x2[j, half]
                for v in range(4):
                    near_out[j, v, half * 32 : half * 32 + 32] = total[v * 32 : v * 32 + 32]
            for v in zl_others:
                near_copy(j, v).start()
            near_in[j, zl] = near_out[j, zl]

    def stage_near(j):
        with jax.named_scope("near"):
            pltpu.make_async_copy(near_in.at[j, pl.ds(0, 3)], near_in.at[j, pl.ds(0, 3)], n_recv.at[j]).wait()
            total = near_in[j, 0] + near_in[j, 1] + near_in[j, 2] + near_in[j, 3]
            for v in range(4):
                for half in range(2):
                    far_out[j, v, half * 8 : half * 8 + 8] = total[half * 32 + v * 8 : half * 32 + v * 8 + 8]
            for v in zh_others:
                far_copy(j, v).start()
            far_in[j, zh] = far_out[j, zh]

    def stage_far(j):
        with jax.named_scope("far"):
            pltpu.make_async_copy(far_in.at[j, pl.ds(0, 3)], far_in.at[j, pl.ds(0, 3)], f_recv.at[j]).wait()
            total = far_in[j, 0] + far_in[j, 1] + far_in[j, 2] + far_in[j, 3]
            for half in range(2):
                g_buf[pl.ds(half * 64 + j, 8, stride=8), :] = total[half * 8 : half * 8 + 8]

    def bias_stage(k):
        if k == 0:

            @pl.when(x == 0)
            def _():
                pltpu.make_async_copy(bias_x.at[pl.ds(1, 3)], bias_x.at[pl.ds(1, 3)], b_recv.at[0]).wait()
                bias_out[1] = bias_out[0] + bias_x[1] + bias_x[2] + bias_x[3]

                @pl.when(zl != 0)
                def _():
                    remote(bias_out.at[1], bias_n.at[zl], b_send.at[1], b_recv.at[1], at(pz=zh * 4)).start()

        elif k == 1:

            @pl.when((x == 0) & (zl == 0))
            def _():
                pltpu.make_async_copy(bias_n.at[pl.ds(1, 3)], bias_n.at[pl.ds(1, 3)], b_recv.at[1]).wait()
                bias_out[2] = bias_out[1] + bias_n[1] + bias_n[2] + bias_n[3]

                @pl.when(zh != 0)
                def _():
                    remote(bias_out.at[2], bias_f.at[zh], b_send.at[2], b_recv.at[2], at(pz=0)).start()

        else:

            @pl.when(dp == 0)
            def _():
                pltpu.make_async_copy(bias_f.at[pl.ds(1, 3)], bias_f.at[pl.ds(1, 3)], b_recv.at[2]).wait()
                rows[0:8] = bias_out[2] + bias_f[1] + bias_f[2] + bias_f[3]

    rows[0:8] = jnp.zeros((8, LANES), jnp.float32)
    stages = [stage_mul, stage_x1, stage_x2, stage_near, stage_far]
    for step in range(CH + len(stages) - 1):
        for lag, stage in enumerate(stages):
            if 0 <= step - lag < CH:
                stage(step - lag)
        if step < 3:
            bias_stage(step)

    def g_copy(k, m):
        src = g_buf.at[pl.ds(pl.multiple_of(((m % NC) * NY + m // NC) * 16, 16), 16)]
        dst = g_in.at[k, pl.ds(pl.multiple_of(mp * 16, 16), 16)]
        return remote(src, dst, g_send, g_recv.at[k], at(p=dp if k == 0 else before, m=m))

    with jax.named_scope("heads"):
        for m in mp_others:
            g_copy(0, m).start()
        for k in range(NMP):
            g_copy(1, (mp + k) % NMP).start()
        own = pl.ds(pl.multiple_of(mp * 16, 16), 16)
        g_in[0, own] = g_buf[pl.ds(pl.multiple_of((c * NY + y) * 16, 16), 16)]
        pltpu.make_async_copy(g_in.at[0, pl.ds(0, 112)], g_in.at[0, pl.ds(0, 112)], g_recv.at[0]).wait()
        pltpu.make_async_copy(g_in.at[1], g_in.at[1], g_recv.at[1]).wait()

    with jax.named_scope("update"):
        for k in range(2):
            for m in range(NMP):
                for e in range(2):
                    start = 8 + k * 80 + e * 40 + CH * m
                    rows[start : start + CH] = g_in[k, m * 16 + e * 8 : m * 16 + e * 8 + CH]
        head_total = jnp.sum(rows[0:8] * rows[0:8]) / 8.0
        head_moment = beta_two * block_ref[NMP * HEAD + mp] + (1.0 - beta_two) * (head_total / HEAD)
        denom[0:8] = jnp.full((8, LANES), head_moment, jnp.float32)
        for k in range(4):
            unit = rows[8 + k * 40 : 48 + k * 40]
            unit_moment = beta_two * block_ref[mp * HEAD + 2 * dp + k] + (1.0 - beta_two) * (
                jnp.sum(unit * unit) / WIDTH
            )
            denom[8 + k * 40 : 48 + k * 40] = jnp.full((40, LANES), unit_moment, jnp.float32)
        grad = rows[pl.ds(dp + 7, ROWS_P), :]
        moment = denom[pl.ds(dp + 7, ROWS_P), :]
        momentum = beta_one * first_ref[0] + (1.0 - beta_one) * grad
        step_dir = momentum / bias_one / (jnp.sqrt(moment / bias_two) + epsilon)
        position = dp * ROWS_P + lax.broadcasted_iota(jnp.int32, (ROWS_P, LANES), 0)
        out_ref[0] = jnp.where(position < USED_ROWS, step_dir, 0.0)

    with jax.named_scope("drain"):
        for v in y_others:
            v_copy(v, mp).wait_send()
        for v in range(NY):
            w_copy(v * NC + c).wait_send()
        for j in range(CH):
            for m in mp_others:
                a_copy(j, m).wait_send()
            for half in range(2):
                for copy in x1_copies(j, half):
                    copy.wait_send()
                x2_copy(j, half).wait_send()
            for v in zl_others:
                near_copy(j, v).wait_send()
            for v in zh_others:
                far_copy(j, v).wait_send()
        for m in mp_others:
            g_copy(0, m).wait_send()
        for m in range(NMP):
            g_copy(1, m).wait_send()

        @pl.when(x != 0)
        def _():
            remote(bias_out.at[0], bias_x.at[x], b_send.at[0], b_recv.at[0], at(px=0)).wait_send()

        @pl.when((x == 0) & (zl != 0))
        def _():
            remote(bias_out.at[1], bias_n.at[zl], b_send.at[1], b_recv.at[1], at(pz=zh * 4)).wait_send()

        @pl.when((x == 0) & (zl == 0) & (zh != 0))
        def _():
            remote(bias_out.at[2], bias_f.at[zh], b_send.at[2], b_recv.at[2], at(pz=0)).wait_send()


def body(value_grads, activations, block_moment, first_moment):
    f32, bf16 = jnp.float32, jnp.bfloat16
    dma = pltpu.SemaphoreType.DMA
    vmem = pl.BlockSpec(memory_space=pltpu.VMEM)
    return pl.pallas_call(
        kernel,
        out_shape=jax.ShapeDtypeStruct(first_moment.shape, f32),
        in_specs=[
            vmem,
            vmem,
            pl.BlockSpec(memory_space=pl.ANY),
            pl.BlockSpec(memory_space=pltpu.SMEM),
            vmem,
        ],
        out_specs=vmem,
        scratch_shapes=[
            pltpu.VMEM((NMP, HEAD, TOKENS), bf16),
            pltpu.VMEM((CH, TOKENS, LANES), bf16),
            pltpu.VMEM((CH, 2, 512, LANES), f32),
            pltpu.VMEM((CH, 2, 2, 128, LANES), f32),
            pltpu.VMEM((CH, 2, 128, LANES), f32),
            pltpu.VMEM((CH, 2, 128, LANES), f32),
            pltpu.VMEM((CH, 4, 64, LANES), f32),
            pltpu.VMEM((CH, 4, 64, LANES), f32),
            pltpu.VMEM((CH, 4, 16, LANES), f32),
            pltpu.VMEM((CH, 4, 16, LANES), f32),
            pltpu.VMEM((128, LANES), f32),
            pltpu.VMEM((2, 128, LANES), f32),
            pltpu.VMEM((168, LANES), f32),
            pltpu.VMEM((168, LANES), f32),
            pltpu.VMEM((3, 8, LANES), f32),
            pltpu.VMEM((4, 8, LANES), f32),
            pltpu.VMEM((4, 8, LANES), f32),
            pltpu.VMEM((4, 8, LANES), f32),
            dma, dma((NMP,)), dma, dma((CH,)), dma((CH,)),
            dma((CH, 2)), dma((CH, 2, 2)), dma((CH, 2)), dma((CH, 2)),
            dma((CH,)), dma((CH,)), dma((CH,)), dma((CH,)),
            dma, dma((2,)), dma((3,)), dma((3,)),
        ],
        compiler_params=pltpu.CompilerParams(
            collective_id=0, has_side_effects=True, vmem_limit_bytes=48 << 20
        ),
        name="gradient_step",
    )(jnp.asarray(unit_order(), bf16), value_grads, activations, block_moment, first_moment)


def solution(mesh):
    return jax.shard_map(
        body,
        mesh=mesh,
        in_specs=(P("dp", "mp"), P(("dp", "mp"), None), P(), P("mp", "dp", None)),
        out_specs=P("mp", "dp", None),
        check_vma=False,
    )
```

```python
import functools

import jax
import jax.numpy as jnp
from jax import lax
from jax.experimental import pallas as pl
from jax.experimental.pallas import tpu as pltpu
from jax.sharding import PartitionSpec as P

MESH = pl.DeviceIdType.MESH

beta_one = 0.9
beta_two = 0.95
bias_one = 1.0 - 0.9**10
bias_two = 1.0 - 0.95**10
epsilon = 1e-08

NX, NZ, NY, NC = 4, 16, 4, 2
NDP, NMP = NX * NZ, NY * NC
LANES = 128
HEAD = 128
TOK = 144
TOKENS = TOK * NMP
WIDTH = 5120
SLICE = WIDTH // NMP
CH = SLICE // LANES
ROWS_P = 81
USED_ROWS = 1 + HEAD * WIDTH // LANES
UNIT_ROWS = WIDTH // LANES


def unit_order():
    r = lax.broadcasted_iota(jnp.int32, (HEAD, HEAD), 0)
    unit = lax.broadcasted_iota(jnp.int32, (HEAD, HEAD), 1)
    e, q = r // 64, r % 64
    p = (q // 16) * 16 + (q % 4) * 4 + (q // 4) % 4
    return jnp.where(unit == 2 * p + e, 1.0, 0.0).astype(jnp.bfloat16)


def kernel(
    vg_hbm, act_ref, block_hbm, first_hbm, out_hbm,
    vg_ref, block_ref, first_ref, out_ref, act_v,
    vt, a_buf, r_buf, x1, s1, x2, near_out, near_in, far_out, far_in, g_buf, g_in, rows, denom,
    bias_out, bias_x, bias_n, bias_f, z_out, z_in, in_sem, act_sem, z_send, z_recv, greet_a, greet_b,
    v_send, v_recv, w_send, a_send, a_recv, x1_send, x1_recv, x2_send, x2_recv,
    n_send, n_recv, f_send, f_recv, g_send, g_recv, b_send, b_recv,
):
    dp, mp = lax.axis_index("dp"), lax.axis_index("mp")
    x, z = dp // NZ, dp % NZ
    zh, zl = z // 4, z % 4
    y, c = mp // NC, mp % NC

    def at(px=None, pz=None, m=None, p=None):
        if p is None:
            p = (x if px is None else px) * NZ + (z if pz is None else pz)
        return {"dp": p, "mp": mp if m is None else m}

    def remote(src, dst, send, recv, device):
        return pltpu.make_async_remote_copy(
            src_ref=src, dst_ref=dst, send_sem=send, recv_sem=recv, device_id=device, device_id_type=MESH
        )

    mp_others = [(mp + k) % NMP for k in range(1, NMP)]
    y_others = [(y + k) % NY for k in range(1, NY)]
    x_others = [(x + k) % NX for k in range(1, NX)]
    z_others = [(z + k) % NZ for k in range(1, NZ)]
    zl_others = [(zl + k) % 4 for k in range(1, 4)]
    zh_others = [(zh + k) % 4 for k in range(1, 4)]
    before, after = (dp + NDP - 1) % NDP, (dp + 1) % NDP
    odd = x % 2
    pair = x + 1 - 2 * odd
    cross = (x + NX - 1 + 2 * odd) % NX

    def cross_of(v):
        return (v + NX - 1 + 2 * (v % 2)) % NX

    def pair_of(v):
        return v + 1 - 2 * (v % 2)

    load = [
        pltpu.make_async_copy(src, dst, in_sem.at[k])
        for k, (src, dst) in enumerate([(vg_hbm, vg_ref), (block_hbm, block_ref), (first_hbm.at[:, 0], first_ref)])
    ]
    with jax.named_scope("entry"):
        for copy in load:
            copy.start()
        barrier = pltpu.get_barrier_semaphore()
        partners = [at(m=m) for m in mp_others]
        partners += [at(px=v) for v in x_others]
        partners += [at(pz=(z + k) % NZ) for k in (1, 2, 3, 13, 14, 15)]
        partners += [at(p=p, m=m) for p in (before, after) for m in range(NMP)]
        for partner in partners:
            pl.semaphore_signal(barrier, inc=1, device_id=partner, device_id_type=MESH)
        for j in range(CH):
            columns = pl.ds(pl.multiple_of(mp * SLICE + j * LANES, LANES), LANES)
            own = pl.ds(pl.multiple_of(mp * TOK, TOK), TOK)
            pltpu.make_async_copy(act_ref.at[:, columns], a_buf.at[j, own], a_recv.at[j]).start()
            for m in range(NMP):
                columns = pl.ds(m * SLICE + j * LANES, LANES)
                pltpu.make_async_copy(act_ref.at[:, columns], act_v.at[j, m], act_sem.at[j]).start()
    with jax.named_scope("turn"):
        load[0].wait()
        vt[mp] = lax.dot_general(
            unit_order(), vg_ref[...], (((1,), (1,)), ((), ())), preferred_element_type=jnp.float32
        ).astype(jnp.bfloat16)
        bias = jnp.sum(vg_ref[...].astype(jnp.float32), axis=0, keepdims=True)
        bias_out[0] = jnp.broadcast_to(bias, (8, LANES))
    with jax.named_scope("barrier"):
        pl.semaphore_wait(barrier, len(partners))

    up, down, across = y_others[0], y_others[2], y_others[1]

    def v_copy(v, slot, part):
        ref = vt.at[slot, pl.ds(part * 64, 64)]
        return remote(ref, ref, v_send, v_recv.at[slot, part], at(m=v * NC + c))

    def w_copy(slot, part):
        ref = vt.at[slot, pl.ds(part * 64, 64)]
        return remote(ref, ref, w_send, v_recv.at[slot, part], at(m=y * NC + 1 - c))

    def a_copy(j, m):
        own = pl.ds(pl.multiple_of(mp * TOK, TOK), TOK)
        return remote(act_v.at[j, m], a_buf.at[j, own], a_send.at[j], a_recv.at[j], at(m=m))

    def greet(sem, k):
        for to in (k, NZ - k):
            pl.semaphore_signal(sem, inc=1, device_id=at(pz=(z + to) % NZ), device_id_type=MESH)

    greet(greet_a, 3)
    with jax.named_scope("send"):
        for j in range(CH):
            pltpu.make_async_copy(act_v.at[j], act_v.at[j], act_sem.at[j]).wait()
        for part in range(2):
            v_copy(up, mp, part).start()
            v_copy(down, mp, 1 - part).start()
        for part in range(2):
            w_copy(mp, part).start()
        for m in mp_others:
            a_copy(0, m).start()

        @pl.when(x != 0)
        def _():
            remote(bias_out.at[0], bias_x.at[x], b_send.at[0], b_recv.at[0], at(px=0)).start()

    with jax.named_scope("forward"):
        from_down, from_up, opposite = down * NC + c, up * NC + c, across * NC + c
        for slot, part, to in ((from_down, 0, up), (from_up, 1, down)):
            w_copy(slot, part).wait_recv()
            v_copy(to, slot, part).start()
            w_copy(slot, part).start()
        for m in mp_others:
            a_copy(1, m).start()
        pl.semaphore_wait(greet_a, 2)
        greet(greet_b, 6)
        for slot, part in ((from_down, 1), (from_up, 0), (opposite, 0), (opposite, 1)):
            w_copy(slot, part).wait_recv()
            w_copy(slot, part).start()
        for v in range(NY):
            for part in range(2):
                w_copy(v * NC + 1 - c, part).wait_recv()

    def first_of(half):
        return (pair, cross_of(pair)) if half == 0 else (cross, pair_of(cross))

    def second_of(half):
        return cross if half == 0 else pair

    def block(b):
        return pl.ds(pl.multiple_of(b * 128, 128), 128)

    def x1_copies(j, half):
        to, other = first_of(half)
        return [
            remote(r_buf.at[j, half, block(b)], x1.at[j, half, k], x1_send.at[j, half], x1_recv.at[j, half, k], at(px=to))
            for k, b in ((1, other), (0, to))
        ]

    def x2_copy(j, half):
        return remote(s1.at[j, half], x2.at[j, half], x2_send.at[j, half], x2_recv.at[j, half], at(px=second_of(half)))

    def near_copy(j, v):
        return remote(near_out.at[j, v], near_in.at[j, zl], n_send.at[j], n_recv.at[j], at(pz=zh * 4 + v))

    def far_copy(j, v):
        return remote(far_out.at[j, v], far_in.at[j, zh], f_send.at[j], f_recv.at[j], at(pz=v * 4 + zl))

    def z_copy(v):
        return remote(z_out.at[v], z_in.at[z], z_send, z_recv, at(pz=v))

    def stage_mul(j):
        with jax.named_scope("mul"):
            pltpu.make_async_copy(a_buf.at[j], a_buf.at[j], a_recv.at[j]).wait()
            if j + 2 < CH:
                for m in mp_others:
                    a_copy(j + 2, m).start()
            for half in range(2):
                for v in range(NY):
                    res = jnp.dot(vt[v * NC + half], a_buf[j], preferred_element_type=jnp.float32)
                    for e in range(2):
                        r_buf[j, half, pl.ds(v * 2 + e, 64, stride=8), :] = res[e * 64 : (e + 1) * 64]
                for copy in x1_copies(j, half):
                    copy.start()

    def stage_x1(j):
        with jax.named_scope("x1"):
            for half in range(2):
                copies = x1_copies(j, half)
                copies[0].wait_recv()
                s1[j, half] = r_buf[j, half, block(second_of(half))] + x1[j, half, 1]
                x2_copy(j, half).start()
            for half in range(2):
                x1_copies(j, half)[1].wait_recv()

    def stage_x2(j):
        with jax.named_scope("x2"):
            for half in range(2):
                x2_copy(j, half).wait_recv()
                total = r_buf[j, half, block(x)] + x1[j, half, 0] + x2[j, half]
                for v in range(4):
                    if j < CH - 1:
                        near_out[j, v, half * 32 : half * 32 + 32] = total[v * 32 : v * 32 + 32]
                    else:
                        for w in range(4):
                            z_out[w * 4 + v, half * 8 : half * 8 + 8] = total[v * 32 + w * 8 : v * 32 + w * 8 + 8]
            if j < CH - 1:
                for v in zl_others:
                    near_copy(j, v).start()
                near_in[j, zl] = near_out[j, zl]
            else:
                for v in z_others:
                    z_copy(v).start()
                z_in[z] = z_out[z]

    def stage_near(j):
        with jax.named_scope("near"):
            pltpu.make_async_copy(near_in.at[j, pl.ds(0, 3)], near_in.at[j, pl.ds(0, 3)], n_recv.at[j]).wait()
            total = near_in[j, 0] + near_in[j, 1] + near_in[j, 2] + near_in[j, 3]
            for v in range(4):
                for half in range(2):
                    far_out[j, v, half * 8 : half * 8 + 8] = total[half * 32 + v * 8 : half * 32 + v * 8 + 8]
            for v in zh_others:
                far_copy(j, v).start()
            far_in[j, zh] = far_out[j, zh]

    def stage_far(j):
        with jax.named_scope("far"):
            pltpu.make_async_copy(far_in.at[j, pl.ds(0, 3)], far_in.at[j, pl.ds(0, 3)], f_recv.at[j]).wait()
            total = far_in[j, 0] + far_in[j, 1] + far_in[j, 2] + far_in[j, 3]
            keep(j, total)

    def stage_z(j):
        with jax.named_scope("z"):
            pltpu.make_async_copy(z_in.at[pl.ds(0, 15)], z_in.at[pl.ds(0, 15)], z_recv).wait()
            keep(j, functools.reduce(jnp.add, [z_in[v] for v in range(NZ)]))

    def keep(j, total):
        for half in range(2):
            g_buf[pl.ds(half * 64 + j, 8, stride=8), :] = total[half * 8 : half * 8 + 8]

    def bias_stage(k):
        if k == 0:

            @pl.when(x == 0)
            def _():
                pltpu.make_async_copy(bias_x.at[pl.ds(1, 3)], bias_x.at[pl.ds(1, 3)], b_recv.at[0]).wait()
                bias_out[1] = bias_out[0] + bias_x[1] + bias_x[2] + bias_x[3]

                @pl.when(zl != 0)
                def _():
                    remote(bias_out.at[1], bias_n.at[zl], b_send.at[1], b_recv.at[1], at(pz=zh * 4)).start()

        elif k == 1:

            @pl.when((x == 0) & (zl == 0))
            def _():
                pltpu.make_async_copy(bias_n.at[pl.ds(1, 3)], bias_n.at[pl.ds(1, 3)], b_recv.at[1]).wait()
                bias_out[2] = bias_out[1] + bias_n[1] + bias_n[2] + bias_n[3]

                @pl.when(zh != 0)
                def _():
                    remote(bias_out.at[2], bias_f.at[zh], b_send.at[2], b_recv.at[2], at(pz=0)).start()

        else:

            @pl.when(dp == 0)
            def _():
                pltpu.make_async_copy(bias_f.at[pl.ds(1, 3)], bias_f.at[pl.ds(1, 3)], b_recv.at[2]).wait()
                rows[0:8] = bias_out[2] + bias_f[1] + bias_f[2] + bias_f[3]

    rows[0:8] = jnp.zeros((8, LANES), jnp.float32)
    lags = [(stage_mul, 0), (stage_x1, 1), (stage_x2, 2), (stage_near, 4)]
    for step in range(CH + 3):
        for stage, lag in lags:
            if 0 <= step - lag < (CH - 1 if stage is stage_near else CH):
                stage(step - lag)
        if step in (1, 3):
            bias_stage(step // 2)
        if step == 2:
            pl.semaphore_wait(greet_b, 2)
    bias_stage(2)
    for j in range(CH - 1):
        stage_far(j)
    stage_z(CH - 1)

    def g_copy(k, m):
        src = g_buf.at[pl.ds(pl.multiple_of(((m % NC) * NY + m // NC) * 16, 16), 16)]
        dst = g_in.at[k, pl.ds(pl.multiple_of(mp * 16, 16), 16)]
        return remote(src, dst, g_send, g_recv.at[k], at(p=dp if k == 0 else before, m=m))

    with jax.named_scope("heads"):
        for m in mp_others:
            g_copy(0, m).start()
        for k in range(NMP):
            g_copy(1, (mp + k) % NMP).start()
        own = pl.ds(pl.multiple_of(mp * 16, 16), 16)
        g_in[0, own] = g_buf[pl.ds(pl.multiple_of((c * NY + y) * 16, 16), 16)]
        pltpu.make_async_copy(g_in.at[0, pl.ds(0, 112)], g_in.at[0, pl.ds(0, 112)], g_recv.at[0]).wait()
        pltpu.make_async_copy(g_in.at[1], g_in.at[1], g_recv.at[1]).wait()

    with jax.named_scope("update"):
        load[1].wait()
        load[2].wait()
        for k in range(2):
            for m in range(NMP):
                for e in range(2):
                    start = 8 + k * 80 + e * 40 + CH * m
                    rows[start : start + CH] = g_in[k, m * 16 + e * 8 : m * 16 + e * 8 + CH]
        head_total = jnp.sum(rows[0:8] * rows[0:8]) / 8.0
        head_moment = beta_two * block_ref[NMP * HEAD + mp] + (1.0 - beta_two) * (head_total / HEAD)
        denom[0:8] = jnp.full((8, LANES), head_moment, jnp.float32)
        for k in range(4):
            unit = rows[8 + k * 40 : 48 + k * 40]
            unit_moment = beta_two * block_ref[mp * HEAD + 2 * dp + k] + (1.0 - beta_two) * (
                jnp.sum(unit * unit) / WIDTH
            )
            denom[8 + k * 40 : 48 + k * 40] = jnp.full((40, LANES), unit_moment, jnp.float32)
        grad = rows[pl.ds(dp + 7, ROWS_P), :]
        moment = denom[pl.ds(dp + 7, ROWS_P), :]
        momentum = beta_one * first_ref[...] + (1.0 - beta_one) * grad
        step_dir = momentum / bias_one / (jnp.sqrt(moment / bias_two) + epsilon)
        position = dp * ROWS_P + lax.broadcasted_iota(jnp.int32, (ROWS_P, LANES), 0)
        out_ref[...] = jnp.where(position < USED_ROWS, step_dir, 0.0)
        store = pltpu.make_async_copy(out_ref, out_hbm.at[:, 0], in_sem.at[3])
        store.start()

    with jax.named_scope("drain"):
        store.wait()
        for part in range(2):
            v_copy(up, mp, part).wait_send()
            v_copy(down, mp, part).wait_send()
        v_copy(up, from_down, 0).wait_send()
        v_copy(down, from_up, 1).wait_send()
        for v in range(NY):
            for part in range(2):
                w_copy(v * NC + c, part).wait_send()
        for j in range(CH):
            for m in mp_others:
                a_copy(j, m).wait_send()
            for half in range(2):
                for copy in x1_copies(j, half):
                    copy.wait_send()
                x2_copy(j, half).wait_send()
        for j in range(CH - 1):
            for v in zl_others:
                near_copy(j, v).wait_send()
            for v in zh_others:
                far_copy(j, v).wait_send()
        for v in z_others:
            z_copy(v).wait_send()
        for m in mp_others:
            g_copy(0, m).wait_send()
        for m in range(NMP):
            g_copy(1, m).wait_send()

        @pl.when(x != 0)
        def _():
            remote(bias_out.at[0], bias_x.at[x], b_send.at[0], b_recv.at[0], at(px=0)).wait_send()

        @pl.when((x == 0) & (zl != 0))
        def _():
            remote(bias_out.at[1], bias_n.at[zl], b_send.at[1], b_recv.at[1], at(pz=zh * 4)).wait_send()

        @pl.when((x == 0) & (zl == 0) & (zh != 0))
        def _():
            remote(bias_out.at[2], bias_f.at[zh], b_send.at[2], b_recv.at[2], at(pz=0)).wait_send()


def body(value_grads, activations, block_moment, first_moment):
    f32, bf16 = jnp.float32, jnp.bfloat16
    dma = pltpu.SemaphoreType.DMA
    update = pl.pallas_call(
        kernel,
        out_shape=jax.ShapeDtypeStruct((ROWS_P, 1, LANES), f32),
        in_specs=[pl.BlockSpec(memory_space=pltpu.HBM)] * 4,
        out_specs=pl.BlockSpec(memory_space=pltpu.HBM),
        scratch_shapes=[
            pltpu.VMEM(value_grads.shape, bf16),
            pltpu.SMEM(block_moment.shape, f32),
            pltpu.VMEM((ROWS_P, LANES), f32),
            pltpu.VMEM((ROWS_P, LANES), f32),
            pltpu.VMEM((CH, NMP, TOK, LANES), bf16),
            pltpu.VMEM((NMP, HEAD, TOKENS), bf16),
            pltpu.VMEM((CH, TOKENS, LANES), bf16),
            pltpu.VMEM((CH, 2, 512, LANES), f32),
            pltpu.VMEM((CH, 2, 2, 128, LANES), f32),
            pltpu.VMEM((CH, 2, 128, LANES), f32),
            pltpu.VMEM((CH, 2, 128, LANES), f32),
            pltpu.VMEM((CH, 4, 64, LANES), f32),
            pltpu.VMEM((CH, 4, 64, LANES), f32),
            pltpu.VMEM((CH, 4, 16, LANES), f32),
            pltpu.VMEM((CH, 4, 16, LANES), f32),
            pltpu.VMEM((128, LANES), f32),
            pltpu.VMEM((2, 128, LANES), f32),
            pltpu.VMEM((168, LANES), f32),
            pltpu.VMEM((168, LANES), f32),
            pltpu.VMEM((3, 8, LANES), f32),
            pltpu.VMEM((4, 8, LANES), f32),
            pltpu.VMEM((4, 8, LANES), f32),
            pltpu.VMEM((4, 8, LANES), f32),
            pltpu.VMEM((NZ, 16, LANES), f32),
            pltpu.VMEM((NZ, 16, LANES), f32),
            dma((4,)), dma((CH,)), dma, dma,
            pltpu.SemaphoreType.REGULAR, pltpu.SemaphoreType.REGULAR,
            dma, dma((NMP, 2)), dma, dma((CH,)), dma((CH,)),
            dma((CH, 2)), dma((CH, 2, 2)), dma((CH, 2)), dma((CH, 2)),
            dma((CH,)), dma((CH,)), dma((CH,)), dma((CH,)),
            dma, dma((2,)), dma((3,)), dma((3,)),
        ],
        compiler_params=pltpu.CompilerParams(
            collective_id=0, has_side_effects=True, vmem_limit_bytes=63 << 20
        ),
        name="gradient_step",
    )(value_grads, activations, block_moment, first_moment.reshape(ROWS_P, 1, LANES))
    return update.reshape(first_moment.shape)


def solution(mesh):
    return jax.shard_map(
        body,
        mesh=mesh,
        in_specs=(P("dp", "mp"), P(("dp", "mp"), None), P(), P("mp", "dp", None)),
        out_specs=P("mp", "dp", None),
        check_vma=False,
    )
```

```python
import functools

import jax
import jax.numpy as jnp
from jax import lax
from jax.experimental import pallas as pl
from jax.experimental.pallas import tpu as pltpu
from jax.sharding import PartitionSpec as P

MESH = pl.DeviceIdType.MESH

beta_one = 0.9
beta_two = 0.95
bias_one = 1.0 - 0.9**10
bias_two = 1.0 - 0.95**10
epsilon = 1e-08

NX, NZ, NY, NC = 4, 16, 4, 2
NDP, NMP = NX * NZ, NY * NC
LANES = 128
HEAD = 128
TOK = 144
TOKENS = TOK * NMP
WIDTH = 5120
SLICE = WIDTH // NMP
CH = SLICE // LANES
STEPS = CH - 1
ROWS_P = 81
USED_ROWS = 1 + HEAD * WIDTH // LANES
UNIT_ROWS = WIDTH // LANES


FAR_FIRST = sorted(range(1, NZ), key=lambda k: -min(k, NZ - k))


def unit_order():
    r = lax.broadcasted_iota(jnp.int32, (HEAD, HEAD), 0)
    unit = lax.broadcasted_iota(jnp.int32, (HEAD, HEAD), 1)
    e, q = r // 64, r % 64
    p = (q // 16) * 16 + (q % 4) * 4 + (q // 4) % 4
    return jnp.where(unit == 2 * p + e, 1.0, 0.0).astype(jnp.bfloat16)


def kernel(
    vg_hbm, act_ref, block_hbm, first_hbm, out_hbm,
    vg_ref, block_ref, first_ref, out_ref, act_v,
    vt, a_buf, r_buf, x1, s1, x2, near_out, near_in, far_out, far_in, g_buf, g_in, rows, denom,
    bias_out, bias_x, bias_n, bias_f, z_out, z_in, in_sem, act_sem, z_send, z_recv, greet_a, greet_b,
    v_send, v_recv, w_send, a_send, a_recv, x1_send, x1_recv, x2_send, x2_recv,
    n_send, n_recv, f_send, f_recv, g_send, g_recv, b_send, b_recv,
):
    dp, mp = lax.axis_index("dp"), lax.axis_index("mp")
    x, z = dp // NZ, dp % NZ
    zh, zl = z // 4, z % 4
    y, c = mp // NC, mp % NC

    def at(px=None, pz=None, m=None, p=None):
        if p is None:
            p = (x if px is None else px) * NZ + (z if pz is None else pz)
        return {"dp": p, "mp": mp if m is None else m}

    def remote(src, dst, send, recv, device):
        return pltpu.make_async_remote_copy(
            src_ref=src, dst_ref=dst, send_sem=send, recv_sem=recv, device_id=device, device_id_type=MESH
        )

    mp_others = [(mp + k) % NMP for k in (4, 3, 5, 2, 6, 1, 7)]
    y_others = [(y + k) % NY for k in range(1, NY)]
    x_others = [(x + k) % NX for k in range(1, NX)]
    z_others = [(z + k) % NZ for k in FAR_FIRST]
    zl_others = [(zl + k) % 4 for k in range(1, 4)]
    zh_others = [(zh + k) % 4 for k in (2, 1, 3)]
    before, after = (dp + NDP - 1) % NDP, (dp + 1) % NDP
    odd = x % 2
    pair = x + 1 - 2 * odd
    cross = (x + NX - 1 + 2 * odd) % NX

    def cross_of(v):
        return (v + NX - 1 + 2 * (v % 2)) % NX

    def pair_of(v):
        return v + 1 - 2 * (v % 2)

    load = [
        pltpu.make_async_copy(src, dst, in_sem.at[k])
        for k, (src, dst) in enumerate([(vg_hbm, vg_ref), (block_hbm, block_ref), (first_hbm.at[:, 0], first_ref)])
    ]
    def load_chunk(j):
        columns = pl.ds(pl.multiple_of(mp * SLICE + j * LANES, LANES), LANES)
        own = pl.ds(pl.multiple_of(mp * TOK, TOK), TOK)
        pltpu.make_async_copy(act_ref.at[:, columns], a_buf.at[j, own], a_recv.at[j]).start()
        for m in range(NMP):
            columns = pl.ds(m * SLICE + j * LANES, LANES)
            pltpu.make_async_copy(act_ref.at[:, columns], act_v.at[j, m], act_sem.at[j]).start()

    def send_chunk(j):
        pltpu.make_async_copy(act_v.at[j], act_v.at[j], act_sem.at[j]).wait()
        for m in mp_others:
            a_copy(j, m).start()

    with jax.named_scope("entry"):
        for copy in load:
            copy.start()
        barrier = pltpu.get_barrier_semaphore()
        partners = [at(m=m) for m in mp_others]
        partners += [at(px=v) for v in x_others]
        partners += [at(pz=(z + k) % NZ) for k in (1, 2, 3, 13, 14, 15)]
        partners += [at(p=p, m=m) for p in (before, after) for m in range(NMP)]
        for partner in partners:
            pl.semaphore_signal(barrier, inc=1, device_id=partner, device_id_type=MESH)
        load_chunk(0)
    with jax.named_scope("turn"):
        load[0].wait()
        vt[mp] = lax.dot_general(
            unit_order(), vg_ref[...], (((1,), (1,)), ((), ())), preferred_element_type=jnp.float32
        ).astype(jnp.bfloat16)
        bias = jnp.sum(vg_ref[...].astype(jnp.float32), axis=0, keepdims=True)
        bias_out[0] = jnp.broadcast_to(bias, (8, LANES))
    with jax.named_scope("barrier"):
        pl.semaphore_wait(barrier, len(partners))

    up, down, across = y_others[0], y_others[2], y_others[1]

    def v_copy(v, slot, part):
        ref = vt.at[slot, pl.ds(part * 64, 64)]
        return remote(ref, ref, v_send, v_recv.at[slot, part], at(m=v * NC + c))

    def w_copy(slot, part):
        ref = vt.at[slot, pl.ds(part * 64, 64)]
        return remote(ref, ref, w_send, v_recv.at[slot, part], at(m=y * NC + 1 - c))

    def a_copy(j, m):
        own = pl.ds(pl.multiple_of(mp * TOK, TOK), TOK)
        return remote(act_v.at[j, m], a_buf.at[j, own], a_send.at[j], a_recv.at[j], at(m=m))

    def greet(sem, k):
        for to in (k, NZ - k):
            pl.semaphore_signal(sem, inc=1, device_id=at(pz=(z + to) % NZ), device_id_type=MESH)

    with jax.named_scope("send"):
        for part in range(2):
            v_copy(up, mp, part).start()
            v_copy(down, mp, 1 - part).start()
        for part in range(2):
            w_copy(mp, part).start()
        send_chunk(0)
        greet(greet_a, 3)
        for j in range(1, CH):
            load_chunk(j)

        @pl.when(x != 0)
        def _():
            remote(bias_out.at[0], bias_x.at[x], b_send.at[0], b_recv.at[0], at(px=0)).start()

    with jax.named_scope("forward"):
        from_down, from_up, opposite = down * NC + c, up * NC + c, across * NC + c
        for slot, part, to in ((from_down, 0, up), (from_up, 1, down)):
            w_copy(slot, part).wait_recv()
            v_copy(to, slot, part).start()
            w_copy(slot, part).start()
        send_chunk(1)
        pl.semaphore_wait(greet_a, 2)
        greet(greet_b, 6)
        for slot, part in ((from_down, 1), (from_up, 0), (opposite, 0), (opposite, 1)):
            w_copy(slot, part).wait_recv()
            w_copy(slot, part).start()
        for v in range(NY):
            for part in range(2):
                w_copy(v * NC + 1 - c, part).wait_recv()

    def first_of(half):
        return (pair, cross_of(pair)) if half == 0 else (cross, pair_of(cross))

    def second_of(half):
        return cross if half == 0 else pair

    def block(b):
        return pl.ds(pl.multiple_of(b * 128, 128), 128)

    def x1_copies(j, half):
        to, other = first_of(half)
        return [
            remote(r_buf.at[j, half, block(b)], x1.at[j, half, k], x1_send.at[j, half], x1_recv.at[j, half, k], at(px=to))
            for k, b in ((1, other), (0, to))
        ]

    def x2_copy(j, half):
        return remote(s1.at[j, half], x2.at[j, half], x2_send.at[j, half], x2_recv.at[j, half], at(px=second_of(half)))

    def near_copy(j, v):
        return remote(near_out.at[j, v], near_in.at[j, zl], n_send.at[j], n_recv.at[j], at(pz=zh * 4 + v))

    def far_copy(j, v):
        return remote(far_out.at[j, v], far_in.at[j, zh], f_send.at[j], f_recv.at[j], at(pz=v * 4 + zl))

    def z_copy(j, v):
        return remote(z_out.at[j - STEPS, v], z_in.at[j - STEPS, z], z_send.at[j - STEPS], z_recv.at[j - STEPS], at(pz=v))

    def stage_mul(j):
        with jax.named_scope("mul"):
            pltpu.make_async_copy(a_buf.at[j], a_buf.at[j], a_recv.at[j]).wait()
            if j + 2 < CH:
                send_chunk(j + 2)
            for half in range(2):
                for v in range(NY):
                    res = jnp.dot(vt[v * NC + half], a_buf[j], preferred_element_type=jnp.float32)
                    for e in range(2):
                        r_buf[j, half, pl.ds(v * 2 + e, 64, stride=8), :] = res[e * 64 : (e + 1) * 64]
                for copy in x1_copies(j, half):
                    copy.start()

    def stage_x1(j):
        with jax.named_scope("x1"):
            for half in range(2):
                copies = x1_copies(j, half)
                copies[0].wait_recv()
                s1[j, half] = r_buf[j, half, block(second_of(half))] + x1[j, half, 1]
                x2_copy(j, half).start()
            for half in range(2):
                x1_copies(j, half)[1].wait_recv()

    def stage_x2(j):
        with jax.named_scope("x2"):
            for half in range(2):
                x2_copy(j, half).wait_recv()
                total = r_buf[j, half, block(x)] + x1[j, half, 0] + x2[j, half]
                for v in range(4):
                    if j < STEPS:
                        near_out[j, v, half * 32 : half * 32 + 32] = total[v * 32 : v * 32 + 32]
                    else:
                        for w in range(4):
                            z_out[j - STEPS, w * 4 + v, half * 8 : half * 8 + 8] = total[v * 32 + w * 8 : v * 32 + w * 8 + 8]
            if j < STEPS:
                for v in zl_others:
                    near_copy(j, v).start()
                near_in[j, zl] = near_out[j, zl]
            else:
                for v in z_others:
                    z_copy(j, v).start()
                z_in[j - STEPS, z] = z_out[j - STEPS, z]

    def stage_near(j):
        with jax.named_scope("near"):
            pltpu.make_async_copy(near_in.at[j, pl.ds(0, 3)], near_in.at[j, pl.ds(0, 3)], n_recv.at[j]).wait()
            total = near_in[j, 0] + near_in[j, 1] + near_in[j, 2] + near_in[j, 3]
            for v in range(4):
                for half in range(2):
                    far_out[j, v, half * 8 : half * 8 + 8] = total[half * 32 + v * 8 : half * 32 + v * 8 + 8]
            for v in zh_others:
                far_copy(j, v).start()
            far_in[j, zh] = far_out[j, zh]

    def stage_far(j):
        with jax.named_scope("far"):
            pltpu.make_async_copy(far_in.at[j, pl.ds(0, 3)], far_in.at[j, pl.ds(0, 3)], f_recv.at[j]).wait()
            total = far_in[j, 0] + far_in[j, 1] + far_in[j, 2] + far_in[j, 3]
            keep(j, total)

    def stage_z(j):
        with jax.named_scope("z"):
            got = z_in.at[j - STEPS, pl.ds(0, NZ - 1)]
            pltpu.make_async_copy(got, got, z_recv.at[j - STEPS]).wait()
            keep(j, functools.reduce(jnp.add, [z_in[j - STEPS, v] for v in range(NZ)]))

    def keep(j, total):
        for half in range(2):
            g_buf[pl.ds(half * 64 + j, 8, stride=8), :] = total[half * 8 : half * 8 + 8]

    def bias_stage(k):
        if k == 0:

            @pl.when(x == 0)
            def _():
                pltpu.make_async_copy(bias_x.at[pl.ds(1, 3)], bias_x.at[pl.ds(1, 3)], b_recv.at[0]).wait()
                bias_out[1] = bias_out[0] + bias_x[1] + bias_x[2] + bias_x[3]

                @pl.when(zl != 0)
                def _():
                    remote(bias_out.at[1], bias_n.at[zl], b_send.at[1], b_recv.at[1], at(pz=zh * 4)).start()

        elif k == 1:

            @pl.when((x == 0) & (zl == 0))
            def _():
                pltpu.make_async_copy(bias_n.at[pl.ds(1, 3)], bias_n.at[pl.ds(1, 3)], b_recv.at[1]).wait()
                bias_out[2] = bias_out[1] + bias_n[1] + bias_n[2] + bias_n[3]

                @pl.when(zh != 0)
                def _():
                    remote(bias_out.at[2], bias_f.at[zh], b_send.at[2], b_recv.at[2], at(pz=0)).start()

        else:

            @pl.when(dp == 0)
            def _():
                pltpu.make_async_copy(bias_f.at[pl.ds(1, 3)], bias_f.at[pl.ds(1, 3)], b_recv.at[2]).wait()
                rows[0:8] = bias_out[2] + bias_f[1] + bias_f[2] + bias_f[3]

    rows[0:8] = jnp.zeros((8, LANES), jnp.float32)
    lags = [(stage_mul, 0), (stage_x1, 1), (stage_x2, 2), (stage_near, 3)]
    for step in range(CH + 3):
        for stage, lag in lags:
            if 0 <= step - lag < (STEPS if stage is stage_near else CH):
                stage(step - lag)
        if step in (1, 3):
            bias_stage(step // 2)
        if step == 2:
            pl.semaphore_wait(greet_b, 2)
    bias_stage(2)
    for j in range(STEPS):
        stage_far(j)
    for j in range(STEPS, CH):
        stage_z(j)

    def g_copy(k, m):
        src = g_buf.at[pl.ds(pl.multiple_of(((m % NC) * NY + m // NC) * 16, 16), 16)]
        dst = g_in.at[k, pl.ds(pl.multiple_of(mp * 16, 16), 16)]
        return remote(src, dst, g_send, g_recv.at[k], at(p=dp if k == 0 else before, m=m))

    with jax.named_scope("heads"):
        for m in mp_others + [mp]:
            g_copy(1, m).start()
        for m in mp_others:
            g_copy(0, m).start()
        own = pl.ds(pl.multiple_of(mp * 16, 16), 16)
        g_in[0, own] = g_buf[pl.ds(pl.multiple_of((c * NY + y) * 16, 16), 16)]
        pltpu.make_async_copy(g_in.at[0, pl.ds(0, 112)], g_in.at[0, pl.ds(0, 112)], g_recv.at[0]).wait()
        pltpu.make_async_copy(g_in.at[1], g_in.at[1], g_recv.at[1]).wait()

    with jax.named_scope("update"):
        load[1].wait()
        load[2].wait()
        for k in range(2):
            for m in range(NMP):
                for e in range(2):
                    start = 8 + k * 80 + e * 40 + CH * m
                    rows[start : start + CH] = g_in[k, m * 16 + e * 8 : m * 16 + e * 8 + CH]
        head_total = jnp.sum(rows[0:8] * rows[0:8]) / 8.0
        head_moment = beta_two * block_ref[NMP * HEAD + mp] + (1.0 - beta_two) * (head_total / HEAD)
        denom[0:8] = jnp.full((8, LANES), head_moment, jnp.float32)
        for k in range(4):
            unit = rows[8 + k * 40 : 48 + k * 40]
            unit_moment = beta_two * block_ref[mp * HEAD + 2 * dp + k] + (1.0 - beta_two) * (
                jnp.sum(unit * unit) / WIDTH
            )
            denom[8 + k * 40 : 48 + k * 40] = jnp.full((40, LANES), unit_moment, jnp.float32)
        grad = rows[pl.ds(dp + 7, ROWS_P), :]
        moment = denom[pl.ds(dp + 7, ROWS_P), :]
        momentum = beta_one * first_ref[...] + (1.0 - beta_one) * grad
        step_dir = momentum / bias_one / (jnp.sqrt(moment / bias_two) + epsilon)
        position = dp * ROWS_P + lax.broadcasted_iota(jnp.int32, (ROWS_P, LANES), 0)
        out_ref[...] = jnp.where(position < USED_ROWS, step_dir, 0.0)
        store = pltpu.make_async_copy(out_ref, out_hbm.at[:, 0], in_sem.at[3])
        store.start()

    with jax.named_scope("drain"):
        store.wait()
        for part in range(2):
            v_copy(up, mp, part).wait_send()
            v_copy(down, mp, part).wait_send()
        v_copy(up, from_down, 0).wait_send()
        v_copy(down, from_up, 1).wait_send()
        for v in range(NY):
            for part in range(2):
                w_copy(v * NC + c, part).wait_send()
        for j in range(CH):
            for m in mp_others:
                a_copy(j, m).wait_send()
            for half in range(2):
                for copy in x1_copies(j, half):
                    copy.wait_send()
                x2_copy(j, half).wait_send()
        for j in range(STEPS):
            for v in zl_others:
                near_copy(j, v).wait_send()
            for v in zh_others:
                far_copy(j, v).wait_send()
        for j in range(STEPS, CH):
            for v in z_others:
                z_copy(j, v).wait_send()
        for m in mp_others:
            g_copy(0, m).wait_send()
        for m in range(NMP):
            g_copy(1, m).wait_send()

        @pl.when(x != 0)
        def _():
            remote(bias_out.at[0], bias_x.at[x], b_send.at[0], b_recv.at[0], at(px=0)).wait_send()

        @pl.when((x == 0) & (zl != 0))
        def _():
            remote(bias_out.at[1], bias_n.at[zl], b_send.at[1], b_recv.at[1], at(pz=zh * 4)).wait_send()

        @pl.when((x == 0) & (zl == 0) & (zh != 0))
        def _():
            remote(bias_out.at[2], bias_f.at[zh], b_send.at[2], b_recv.at[2], at(pz=0)).wait_send()


def body(value_grads, activations, block_moment, first_moment):
    f32, bf16 = jnp.float32, jnp.bfloat16
    dma = pltpu.SemaphoreType.DMA
    update = pl.pallas_call(
        kernel,
        out_shape=jax.ShapeDtypeStruct((ROWS_P, 1, LANES), f32),
        in_specs=[pl.BlockSpec(memory_space=pltpu.HBM)] * 4,
        out_specs=pl.BlockSpec(memory_space=pltpu.HBM),
        scratch_shapes=[
            pltpu.VMEM(value_grads.shape, bf16),
            pltpu.SMEM(block_moment.shape, f32),
            pltpu.VMEM((ROWS_P, LANES), f32),
            pltpu.VMEM((ROWS_P, LANES), f32),
            pltpu.VMEM((CH, NMP, TOK, LANES), bf16),
            pltpu.VMEM((NMP, HEAD, TOKENS), bf16),
            pltpu.VMEM((CH, TOKENS, LANES), bf16),
            pltpu.VMEM((CH, 2, 512, LANES), f32),
            pltpu.VMEM((CH, 2, 2, 128, LANES), f32),
            pltpu.VMEM((CH, 2, 128, LANES), f32),
            pltpu.VMEM((CH, 2, 128, LANES), f32),
            pltpu.VMEM((CH, 4, 64, LANES), f32),
            pltpu.VMEM((CH, 4, 64, LANES), f32),
            pltpu.VMEM((CH, 4, 16, LANES), f32),
            pltpu.VMEM((CH, 4, 16, LANES), f32),
            pltpu.VMEM((128, LANES), f32),
            pltpu.VMEM((2, 128, LANES), f32),
            pltpu.VMEM((168, LANES), f32),
            pltpu.VMEM((168, LANES), f32),
            pltpu.VMEM((3, 8, LANES), f32),
            pltpu.VMEM((4, 8, LANES), f32),
            pltpu.VMEM((4, 8, LANES), f32),
            pltpu.VMEM((4, 8, LANES), f32),
            pltpu.VMEM((CH - STEPS, NZ, 16, LANES), f32),
            pltpu.VMEM((CH - STEPS, NZ, 16, LANES), f32),
            dma((4,)), dma((CH,)), dma((CH - STEPS,)), dma((CH - STEPS,)),
            pltpu.SemaphoreType.REGULAR, pltpu.SemaphoreType.REGULAR,
            dma, dma((NMP, 2)), dma, dma((CH,)), dma((CH,)),
            dma((CH, 2)), dma((CH, 2, 2)), dma((CH, 2)), dma((CH, 2)),
            dma((CH,)), dma((CH,)), dma((CH,)), dma((CH,)),
            dma, dma((2,)), dma((3,)), dma((3,)),
        ],
        compiler_params=pltpu.CompilerParams(
            collective_id=0, has_side_effects=True, vmem_limit_bytes=63 << 20
        ),
        name="gradient_step",
    )(value_grads, activations, block_moment, first_moment.reshape(ROWS_P, 1, LANES))
    return update.reshape(first_moment.shape)


def solution(mesh):
    return jax.shard_map(
        body,
        mesh=mesh,
        in_specs=(P("dp", "mp"), P(("dp", "mp"), None), P(), P("mp", "dp", None)),
        out_specs=P("mp", "dp", None),
        check_vma=False,
    )
```

```python
import functools

import jax
import jax.numpy as jnp
from jax import lax
from jax.experimental import pallas as pl
from jax.experimental.pallas import tpu as pltpu
from jax.sharding import PartitionSpec as P

MESH = pl.DeviceIdType.MESH

beta_one = 0.9
beta_two = 0.95
bias_one = 1.0 - 0.9**10
bias_two = 1.0 - 0.95**10
epsilon = 1e-08

NX, NZ, NY, NC = 4, 16, 4, 2
NDP, NMP = NX * NZ, NY * NC
LANES = 128
HEAD = 128
TOK = 144
TOKENS = TOK * NMP
WIDTH = 5120
SLICE = WIDTH // NMP
CH = SLICE // LANES
STEPS = CH - 1
ROWS_P = 81
USED_ROWS = 1 + HEAD * WIDTH // LANES
UNIT_ROWS = WIDTH // LANES


FAR_FIRST = sorted(range(1, NZ), key=lambda k: -min(k, NZ - k))


def unit_order():
    r = lax.broadcasted_iota(jnp.int32, (HEAD, HEAD), 0)
    unit = lax.broadcasted_iota(jnp.int32, (HEAD, HEAD), 1)
    e, q = r // 64, r % 64
    p = (q // 16) * 16 + (q % 4) * 4 + (q // 4) % 4
    return jnp.where(unit == 2 * p + e, 1.0, 0.0).astype(jnp.bfloat16)


def kernel(
    vg_hbm, act_ref, block_hbm, first_hbm, out_hbm,
    vg_ref, block_ref, first_ref, out_ref, act_v,
    vt, a_buf, r_buf, x1, s1, x2, near_out, near_in, far_out, far_in, g_buf, g_in, rows, denom,
    bias_out, bias_x, bias_n, bias_f, z_out, z_in, in_sem, act_sem, z_send, z_recv, greet_a, greet_b,
    v_send, v_recv, w_send, a_send, a_recv, x1_send, x1_recv, x2_send, x2_recv,
    n_send, n_recv, f_send, f_recv, g_send, g_recv, b_send, b_recv,
):
    dp, mp = lax.axis_index("dp"), lax.axis_index("mp")
    x, z = dp // NZ, dp % NZ
    zh, zl = z // 4, z % 4
    y, c = mp // NC, mp % NC

    def at(px=None, pz=None, m=None, p=None):
        if p is None:
            p = (x if px is None else px) * NZ + (z if pz is None else pz)
        return {"dp": p, "mp": mp if m is None else m}

    def remote(src, dst, send, recv, device):
        return pltpu.make_async_remote_copy(
            src_ref=src, dst_ref=dst, send_sem=send, recv_sem=recv, device_id=device, device_id_type=MESH
        )

    mp_others = [(mp + k) % NMP for k in (4, 3, 5, 2, 6, 1, 7)]
    y_others = [(y + k) % NY for k in range(1, NY)]
    x_others = [(x + k) % NX for k in range(1, NX)]
    z_others = [(z + k) % NZ for k in FAR_FIRST]
    zl_others = [(zl + k) % 4 for k in range(1, 4)]
    zh_others = [(zh + k) % 4 for k in (2, 1, 3)]
    before, after = (dp + NDP - 1) % NDP, (dp + 1) % NDP
    odd = x % 2
    pair = x + 1 - 2 * odd
    cross = (x + NX - 1 + 2 * odd) % NX

    def cross_of(v):
        return (v + NX - 1 + 2 * (v % 2)) % NX

    def pair_of(v):
        return v + 1 - 2 * (v % 2)

    load = [
        pltpu.make_async_copy(src, dst, in_sem.at[k])
        for k, (src, dst) in enumerate([(vg_hbm, vg_ref), (block_hbm, block_ref), (first_hbm.at[:, 0], first_ref)])
    ]
    def load_chunk(j):
        columns = pl.ds(pl.multiple_of(mp * SLICE + j * LANES, LANES), LANES)
        own = pl.ds(pl.multiple_of(mp * TOK, TOK), TOK)
        pltpu.make_async_copy(act_ref.at[:, columns], a_buf.at[j, own], a_recv.at[j]).start()
        for m in range(NMP):
            columns = pl.ds(m * SLICE + j * LANES, LANES)
            pltpu.make_async_copy(act_ref.at[:, columns], act_v.at[j, m], act_sem.at[j]).start()

    def send_chunk(j):
        pltpu.make_async_copy(act_v.at[j], act_v.at[j], act_sem.at[j]).wait()
        for m in mp_others:
            a_copy(j, m).start()

    with jax.named_scope("entry"):
        for copy in load:
            copy.start()
        barrier = pltpu.get_barrier_semaphore()
        partners = [at(m=m) for m in mp_others]
        partners += [at(px=v) for v in x_others]
        partners += [at(pz=(z + k) % NZ) for k in (1, 2, 3, 13, 14, 15)]
        partners += [at(p=p, m=m) for p in (before, after) for m in range(NMP)]
        for partner in partners:
            pl.semaphore_signal(barrier, inc=1, device_id=partner, device_id_type=MESH)
        load_chunk(0)
    with jax.named_scope("turn"):
        load[0].wait()
        vt[mp] = lax.dot_general(
            unit_order(), vg_ref[...], (((1,), (1,)), ((), ())), preferred_element_type=jnp.float32
        ).astype(jnp.bfloat16)
    with jax.named_scope("barrier"):
        pl.semaphore_wait(barrier, len(partners))

    up, down, across = y_others[0], y_others[2], y_others[1]

    def v_copy(v, slot, part):
        ref = vt.at[slot, pl.ds(part * 64, 64)]
        return remote(ref, ref, v_send, v_recv.at[slot, part], at(m=v * NC + c))

    def w_copy(slot, part):
        ref = vt.at[slot, pl.ds(part * 64, 64)]
        return remote(ref, ref, w_send, v_recv.at[slot, part], at(m=y * NC + 1 - c))

    def a_copy(j, m):
        own = pl.ds(pl.multiple_of(mp * TOK, TOK), TOK)
        return remote(act_v.at[j, m], a_buf.at[j, own], a_send.at[j], a_recv.at[j], at(m=m))

    def greet(sem, k):
        for to in (k, NZ - k):
            pl.semaphore_signal(sem, inc=1, device_id=at(pz=(z + to) % NZ), device_id_type=MESH)

    with jax.named_scope("send"):
        for part in range(2):
            v_copy(up, mp, part).start()
            v_copy(down, mp, 1 - part).start()
        for part in range(2):
            w_copy(mp, part).start()
        send_chunk(0)
        greet(greet_a, 3)
        for j in range(1, CH):
            load_chunk(j)

        bias = jnp.sum(vg_ref[...].astype(jnp.float32), axis=0, keepdims=True)
        bias_out[0] = jnp.broadcast_to(bias, (8, LANES))

        @pl.when(x != 0)
        def _():
            remote(bias_out.at[0], bias_x.at[x], b_send.at[0], b_recv.at[0], at(px=0)).start()

    with jax.named_scope("forward"):
        from_down, from_up, opposite = down * NC + c, up * NC + c, across * NC + c
        for slot, part, to in ((from_down, 0, up), (from_up, 1, down)):
            w_copy(slot, part).wait_recv()
            v_copy(to, slot, part).start()
            w_copy(slot, part).start()
        send_chunk(1)
        pl.semaphore_wait(greet_a, 2)
        greet(greet_b, 6)
        for slot, part in ((from_down, 1), (from_up, 0), (opposite, 0), (opposite, 1)):
            w_copy(slot, part).wait_recv()
            w_copy(slot, part).start()
        for v in range(NY):
            for part in range(2):
                w_copy(v * NC + 1 - c, part).wait_recv()

    def first_of(half):
        return (pair, cross_of(pair)) if half == 0 else (cross, pair_of(cross))

    def second_of(half):
        return cross if half == 0 else pair

    def block(b):
        return pl.ds(pl.multiple_of(b * 128, 128), 128)

    def x1_copies(j, half):
        to, other = first_of(half)
        return [
            remote(r_buf.at[j, half, block(b)], x1.at[j, half, k], x1_send.at[j, half], x1_recv.at[j, half, k], at(px=to))
            for k, b in ((1, other), (0, to))
        ]

    def x2_copy(j, half):
        return remote(s1.at[j, half], x2.at[j, half], x2_send.at[j, half], x2_recv.at[j, half], at(px=second_of(half)))

    def near_copy(j, v):
        return remote(near_out.at[j, v], near_in.at[j, zl], n_send.at[j], n_recv.at[j], at(pz=zh * 4 + v))

    def far_copy(j, v):
        return remote(far_out.at[j, v], far_in.at[j, zh], f_send.at[j], f_recv.at[j], at(pz=v * 4 + zl))

    def z_copy(j, half, v):
        k, part = j - STEPS, pl.ds(half * 8, 8)
        return remote(z_out.at[k, v, part], z_in.at[k, z, part], z_send.at[k], z_recv.at[k], at(pz=v))

    def stage_mul(j):
        with jax.named_scope("mul"):
            pltpu.make_async_copy(a_buf.at[j], a_buf.at[j], a_recv.at[j]).wait()
            if j + 2 < CH:
                send_chunk(j + 2)
            for half in range(2):
                for v in range(NY):
                    res = jnp.dot(vt[v * NC + half], a_buf[j], preferred_element_type=jnp.float32)
                    for e in range(2):
                        r_buf[j, half, pl.ds(v * 2 + e, 64, stride=8), :] = res[e * 64 : (e + 1) * 64]
                for copy in x1_copies(j, half):
                    copy.start()

    def stage_x1(j):
        with jax.named_scope("x1"):
            for half in range(2):
                copies = x1_copies(j, half)
                copies[0].wait_recv()
                s1[j, half] = r_buf[j, half, block(second_of(half))] + x1[j, half, 1]
                x2_copy(j, half).start()
            for half in range(2):
                x1_copies(j, half)[1].wait_recv()

    def stage_x2(j):
        with jax.named_scope("x2"):
            for half in range(2):
                x2_copy(j, half).wait_recv()
                total = r_buf[j, half, block(x)] + x1[j, half, 0] + x2[j, half]
                for v in range(4):
                    if j < STEPS:
                        near_out[j, v, half * 32 : half * 32 + 32] = total[v * 32 : v * 32 + 32]
                    else:
                        for w in range(4):
                            z_out[j - STEPS, w * 4 + v, half * 8 : half * 8 + 8] = total[v * 32 + w * 8 : v * 32 + w * 8 + 8]
                if j >= STEPS:
                    for v in z_others:
                        z_copy(j, half, v).start()
            if j < STEPS:
                for v in zl_others:
                    near_copy(j, v).start()
                near_in[j, zl] = near_out[j, zl]
            else:
                z_in[j - STEPS, z] = z_out[j - STEPS, z]

    def stage_near(j):
        with jax.named_scope("near"):
            pltpu.make_async_copy(near_in.at[j, pl.ds(0, 3)], near_in.at[j, pl.ds(0, 3)], n_recv.at[j]).wait()
            total = near_in[j, 0] + near_in[j, 1] + near_in[j, 2] + near_in[j, 3]
            for v in range(4):
                for half in range(2):
                    far_out[j, v, half * 8 : half * 8 + 8] = total[half * 32 + v * 8 : half * 32 + v * 8 + 8]
            for v in zh_others:
                far_copy(j, v).start()
            far_in[j, zh] = far_out[j, zh]

    def stage_far(j):
        with jax.named_scope("far"):
            pltpu.make_async_copy(far_in.at[j, pl.ds(0, 3)], far_in.at[j, pl.ds(0, 3)], f_recv.at[j]).wait()
            total = far_in[j, 0] + far_in[j, 1] + far_in[j, 2] + far_in[j, 3]
            keep(j, total)

    def stage_z(j):
        with jax.named_scope("z"):
            got = z_in.at[j - STEPS, pl.ds(0, NZ - 1)]
            pltpu.make_async_copy(got, got, z_recv.at[j - STEPS]).wait()
            keep(j, functools.reduce(jnp.add, [z_in[j - STEPS, v] for v in range(NZ)]))

    def keep(j, total):
        for half in range(2):
            g_buf[pl.ds(half * 64 + j, 8, stride=8), :] = total[half * 8 : half * 8 + 8]

    def bias_stage(k):
        if k == 0:

            @pl.when(x == 0)
            def _():
                pltpu.make_async_copy(bias_x.at[pl.ds(1, 3)], bias_x.at[pl.ds(1, 3)], b_recv.at[0]).wait()
                bias_out[1] = bias_out[0] + bias_x[1] + bias_x[2] + bias_x[3]

                @pl.when(zl != 0)
                def _():
                    remote(bias_out.at[1], bias_n.at[zl], b_send.at[1], b_recv.at[1], at(pz=zh * 4)).start()

        elif k == 1:

            @pl.when((x == 0) & (zl == 0))
            def _():
                pltpu.make_async_copy(bias_n.at[pl.ds(1, 3)], bias_n.at[pl.ds(1, 3)], b_recv.at[1]).wait()
                bias_out[2] = bias_out[1] + bias_n[1] + bias_n[2] + bias_n[3]

                @pl.when(zh != 0)
                def _():
                    remote(bias_out.at[2], bias_f.at[zh], b_send.at[2], b_recv.at[2], at(pz=0)).start()

        else:

            @pl.when(dp == 0)
            def _():
                pltpu.make_async_copy(bias_f.at[pl.ds(1, 3)], bias_f.at[pl.ds(1, 3)], b_recv.at[2]).wait()
                rows[0:8] = bias_out[2] + bias_f[1] + bias_f[2] + bias_f[3]

    rows[0:8] = jnp.zeros((8, LANES), jnp.float32)
    lags = [(stage_mul, 0), (stage_x1, 1), (stage_x2, 2), (stage_near, 3)]
    for step in range(CH + 3):
        for stage, lag in lags:
            if 0 <= step - lag < (STEPS if stage is stage_near else CH):
                stage(step - lag)
        if step in (1, 3):
            bias_stage(step // 2)
        if step == 2:
            pl.semaphore_wait(greet_b, 2)
    bias_stage(2)
    with jax.named_scope("sent"):
        for part in range(2):
            v_copy(up, mp, part).wait_send()
            v_copy(down, mp, part).wait_send()
        v_copy(up, from_down, 0).wait_send()
        v_copy(down, from_up, 1).wait_send()
        for v in range(NY):
            for part in range(2):
                w_copy(v * NC + c, part).wait_send()
        for j in range(CH):
            for m in mp_others:
                a_copy(j, m).wait_send()
            for half in range(2):
                for copy in x1_copies(j, half):
                    copy.wait_send()
                x2_copy(j, half).wait_send()
    for j in range(STEPS):
        stage_far(j)
    for j in range(STEPS, CH):
        stage_z(j)

    def g_copy(k, m):
        src = g_buf.at[pl.ds(pl.multiple_of(((m % NC) * NY + m // NC) * 16, 16), 16)]
        dst = g_in.at[k, pl.ds(pl.multiple_of(mp * 16, 16), 16)]
        return remote(src, dst, g_send, g_recv.at[k], at(p=dp if k == 0 else before, m=m))

    with jax.named_scope("heads"):
        for m in mp_others + [mp]:
            g_copy(1, m).start()
        for m in mp_others:
            g_copy(0, m).start()
        own = pl.ds(pl.multiple_of(mp * 16, 16), 16)
        g_in[0, own] = g_buf[pl.ds(pl.multiple_of((c * NY + y) * 16, 16), 16)]
        pltpu.make_async_copy(g_in.at[0, pl.ds(0, 112)], g_in.at[0, pl.ds(0, 112)], g_recv.at[0]).wait()
        pltpu.make_async_copy(g_in.at[1], g_in.at[1], g_recv.at[1]).wait()

    with jax.named_scope("update"):
        load[1].wait()
        load[2].wait()
        for k in range(2):
            for m in range(NMP):
                for e in range(2):
                    start = 8 + k * 80 + e * 40 + CH * m
                    rows[start : start + CH] = g_in[k, m * 16 + e * 8 : m * 16 + e * 8 + CH]
        head_total = jnp.sum(rows[0:8] * rows[0:8]) / 8.0
        head_moment = beta_two * block_ref[NMP * HEAD + mp] + (1.0 - beta_two) * (head_total / HEAD)
        denom[0:8] = jnp.full((8, LANES), head_moment, jnp.float32)
        for k in range(4):
            unit = rows[8 + k * 40 : 48 + k * 40]
            unit_moment = beta_two * block_ref[mp * HEAD + 2 * dp + k] + (1.0 - beta_two) * (
                jnp.sum(unit * unit) / WIDTH
            )
            denom[8 + k * 40 : 48 + k * 40] = jnp.full((40, LANES), unit_moment, jnp.float32)
        grad = rows[pl.ds(dp + 7, ROWS_P), :]
        moment = denom[pl.ds(dp + 7, ROWS_P), :]
        momentum = beta_one * first_ref[...] + (1.0 - beta_one) * grad
        step_dir = momentum / bias_one / (jnp.sqrt(moment / bias_two) + epsilon)
        position = dp * ROWS_P + lax.broadcasted_iota(jnp.int32, (ROWS_P, LANES), 0)
        out_ref[...] = jnp.where(position < USED_ROWS, step_dir, 0.0)
        store = pltpu.make_async_copy(out_ref, out_hbm.at[:, 0], in_sem.at[3])
        store.start()

    with jax.named_scope("drain"):
        store.wait()
        for j in range(STEPS):
            for v in zl_others:
                near_copy(j, v).wait_send()
            for v in zh_others:
                far_copy(j, v).wait_send()
        for j in range(STEPS, CH):
            for v in z_others:
                for half in range(2):
                    z_copy(j, half, v).wait_send()
        for m in mp_others:
            g_copy(0, m).wait_send()
        for m in range(NMP):
            g_copy(1, m).wait_send()

        @pl.when(x != 0)
        def _():
            remote(bias_out.at[0], bias_x.at[x], b_send.at[0], b_recv.at[0], at(px=0)).wait_send()

        @pl.when((x == 0) & (zl != 0))
        def _():
            remote(bias_out.at[1], bias_n.at[zl], b_send.at[1], b_recv.at[1], at(pz=zh * 4)).wait_send()

        @pl.when((x == 0) & (zl == 0) & (zh != 0))
        def _():
            remote(bias_out.at[2], bias_f.at[zh], b_send.at[2], b_recv.at[2], at(pz=0)).wait_send()


def body(value_grads, activations, block_moment, first_moment):
    f32, bf16 = jnp.float32, jnp.bfloat16
    dma = pltpu.SemaphoreType.DMA
    update = pl.pallas_call(
        kernel,
        out_shape=jax.ShapeDtypeStruct((ROWS_P, 1, LANES), f32),
        in_specs=[pl.BlockSpec(memory_space=pltpu.HBM)] * 4,
        out_specs=pl.BlockSpec(memory_space=pltpu.HBM),
        scratch_shapes=[
            pltpu.VMEM(value_grads.shape, bf16),
            pltpu.SMEM(block_moment.shape, f32),
            pltpu.VMEM((ROWS_P, LANES), f32),
            pltpu.VMEM((ROWS_P, LANES), f32),
            pltpu.VMEM((CH, NMP, TOK, LANES), bf16),
            pltpu.VMEM((NMP, HEAD, TOKENS), bf16),
            pltpu.VMEM((CH, TOKENS, LANES), bf16),
            pltpu.VMEM((CH, 2, 512, LANES), f32),
            pltpu.VMEM((CH, 2, 2, 128, LANES), f32),
            pltpu.VMEM((CH, 2, 128, LANES), f32),
            pltpu.VMEM((CH, 2, 128, LANES), f32),
            pltpu.VMEM((CH, 4, 64, LANES), f32),
            pltpu.VMEM((CH, 4, 64, LANES), f32),
            pltpu.VMEM((CH, 4, 16, LANES), f32),
            pltpu.VMEM((CH, 4, 16, LANES), f32),
            pltpu.VMEM((128, LANES), f32),
            pltpu.VMEM((2, 128, LANES), f32),
            pltpu.VMEM((168, LANES), f32),
            pltpu.VMEM((168, LANES), f32),
            pltpu.VMEM((3, 8, LANES), f32),
            pltpu.VMEM((4, 8, LANES), f32),
            pltpu.VMEM((4, 8, LANES), f32),
            pltpu.VMEM((4, 8, LANES), f32),
            pltpu.VMEM((CH - STEPS, NZ, 16, LANES), f32),
            pltpu.VMEM((CH - STEPS, NZ, 16, LANES), f32),
            dma((4,)), dma((CH,)), dma((CH - STEPS,)), dma((CH - STEPS,)),
            pltpu.SemaphoreType.REGULAR, pltpu.SemaphoreType.REGULAR,
            dma, dma((NMP, 2)), dma, dma((CH,)), dma((CH,)),
            dma((CH, 2)), dma((CH, 2, 2)), dma((CH, 2)), dma((CH, 2)),
            dma((CH,)), dma((CH,)), dma((CH,)), dma((CH,)),
            dma, dma((2,)), dma((3,)), dma((3,)),
        ],
        compiler_params=pltpu.CompilerParams(
            collective_id=0, has_side_effects=True, vmem_limit_bytes=63 << 20
        ),
        name="gradient_step",
    )(value_grads, activations, block_moment, first_moment.reshape(ROWS_P, 1, LANES))
    return update.reshape(first_moment.shape)


def solution(mesh):
    return jax.shard_map(
        body,
        mesh=mesh,
        in_specs=(P("dp", "mp"), P(("dp", "mp"), None), P(), P("mp", "dp", None)),
        out_specs=P("mp", "dp", None),
        check_vma=False,
    )
```

```python
import functools

import jax
import jax.numpy as jnp
from jax import lax
from jax.experimental import pallas as pl
from jax.experimental.pallas import tpu as pltpu
from jax.sharding import PartitionSpec as P

MESH = pl.DeviceIdType.MESH

beta_one = 0.9
beta_two = 0.95
bias_one = 1.0 - 0.9**10
bias_two = 1.0 - 0.95**10
epsilon = 1e-08

NX, NZ, NY, NC = 4, 16, 4, 2
NDP, NMP = NX * NZ, NY * NC
LANES = 128
HEAD = 128
TOK = 144
TOKENS = TOK * NMP
WIDTH = 5120
SLICE = WIDTH // NMP
CH = SLICE // LANES
STEPS = CH - 1
ROWS_P = 81
USED_ROWS = 1 + HEAD * WIDTH // LANES
UNIT_ROWS = WIDTH // LANES


FAR_FIRST = sorted(range(1, NZ), key=lambda k: -min(k, NZ - k))


def unit_order():
    r = lax.broadcasted_iota(jnp.int32, (HEAD, HEAD), 0)
    unit = lax.broadcasted_iota(jnp.int32, (HEAD, HEAD), 1)
    e, q = r // 64, r % 64
    p = (q // 16) * 16 + (q % 4) * 4 + (q // 4) % 4
    return jnp.where(unit == 2 * p + e, 1.0, 0.0).astype(jnp.bfloat16)


def kernel(
    vg_hbm, act_ref, block_hbm, first_hbm, out_hbm,
    vg_ref, block_ref, first_ref, out_ref, act_v,
    vt, a_buf, r_buf, x1, s1, x2, near_out, near_in, far_out, far_in, g_buf, g_in, rows, denom,
    bias_out, bias_x, bias_n, bias_f, z_out, z_in, in_sem, act_sem, z_send, z_recv, greet_a, greet_b,
    v_send, v_recv, w_send, a_send, a_recv, x1_send, x1_recv, x2_send, x2_recv,
    n_send, n_recv, f_send, f_recv, g_send, g_recv, b_send, b_recv,
):
    dp, mp = lax.axis_index("dp"), lax.axis_index("mp")
    x, z = dp // NZ, dp % NZ
    zh, zl = z // 4, z % 4
    y, c = mp // NC, mp % NC

    def at(px=None, pz=None, m=None, p=None):
        if p is None:
            p = (x if px is None else px) * NZ + (z if pz is None else pz)
        return {"dp": p, "mp": mp if m is None else m}

    def remote(src, dst, send, recv, device):
        return pltpu.make_async_remote_copy(
            src_ref=src, dst_ref=dst, send_sem=send, recv_sem=recv, device_id=device, device_id_type=MESH
        )

    mp_others = [(mp + k) % NMP for k in (4, 3, 5, 2, 6, 1, 7)]
    y_others = [(y + k) % NY for k in range(1, NY)]
    x_others = [(x + k) % NX for k in range(1, NX)]
    z_others = [(z + k) % NZ for k in FAR_FIRST]
    zl_others = [(zl + k) % 4 for k in range(1, 4)]
    zh_others = [(zh + k) % 4 for k in (2, 1, 3)]
    before, after = (dp + NDP - 1) % NDP, (dp + 1) % NDP
    odd = x % 2
    pair = x + 1 - 2 * odd
    cross = (x + NX - 1 + 2 * odd) % NX

    def cross_of(v):
        return (v + NX - 1 + 2 * (v % 2)) % NX

    def pair_of(v):
        return v + 1 - 2 * (v % 2)

    load = [
        pltpu.make_async_copy(src, dst, in_sem.at[k])
        for k, (src, dst) in enumerate([(vg_hbm, vg_ref), (block_hbm, block_ref), (first_hbm.at[:, 0], first_ref)])
    ]
    def load_chunk(j):
        columns = pl.ds(pl.multiple_of(mp * SLICE + j * LANES, LANES), LANES)
        own = pl.ds(pl.multiple_of(mp * TOK, TOK), TOK)
        pltpu.make_async_copy(act_ref.at[:, columns], a_buf.at[j, own], a_recv.at[j]).start()
        for m in range(NMP):
            columns = pl.ds(m * SLICE + j * LANES, LANES)
            pltpu.make_async_copy(act_ref.at[:, columns], act_v.at[j, m], act_sem.at[j]).start()

    def send_chunk(j):
        pltpu.make_async_copy(act_v.at[j], act_v.at[j], act_sem.at[j]).wait()
        for m in mp_others:
            a_copy(j, m).start()

    with jax.named_scope("entry"):
        for copy in load:
            copy.start()
        barrier = pltpu.get_barrier_semaphore()
        partners = [at(m=m) for m in mp_others]
        partners += [at(px=v) for v in x_others]
        partners += [at(pz=(z + k) % NZ) for k in (1, 2, 3, 13, 14, 15)]
        partners += [at(p=p, m=m) for p in (before, after) for m in range(NMP)]
        for partner in partners:
            pl.semaphore_signal(barrier, inc=1, device_id=partner, device_id_type=MESH)
        load_chunk(0)
    with jax.named_scope("turn"):
        load[0].wait()
        vt[mp] = lax.dot_general(
            unit_order(), vg_ref[...], (((1,), (1,)), ((), ())), preferred_element_type=jnp.float32
        ).astype(jnp.bfloat16)
    with jax.named_scope("barrier"):
        pl.semaphore_wait(barrier, len(partners))

    up, down, across = y_others[0], y_others[2], y_others[1]

    def v_copy(v, slot, part):
        ref = vt.at[slot, pl.ds(part * 64, 64)]
        return remote(ref, ref, v_send, v_recv.at[slot, part], at(m=v * NC + c))

    def w_copy(slot, part):
        ref = vt.at[slot, pl.ds(part * 64, 64)]
        return remote(ref, ref, w_send, v_recv.at[slot, part], at(m=y * NC + 1 - c))

    def a_copy(j, m):
        own = pl.ds(pl.multiple_of(mp * TOK, TOK), TOK)
        return remote(act_v.at[j, m], a_buf.at[j, own], a_send.at[j], a_recv.at[j], at(m=m))

    def greet(sem, k):
        for to in (k, NZ - k):
            pl.semaphore_signal(sem, inc=1, device_id=at(pz=(z + to) % NZ), device_id_type=MESH)

    with jax.named_scope("send"):
        for part in range(2):
            v_copy(up, mp, part).start()
            v_copy(down, mp, 1 - part).start()
        for part in range(2):
            w_copy(mp, part).start()
        send_chunk(0)
        greet(greet_a, 3)
        for j in range(1, CH):
            load_chunk(j)

        bias = jnp.sum(vg_ref[...].astype(jnp.float32), axis=0, keepdims=True)
        bias_out[0] = jnp.broadcast_to(bias, (8, LANES))

        @pl.when(x != 0)
        def _():
            remote(bias_out.at[0], bias_x.at[x], b_send.at[0], b_recv.at[0], at(px=0)).start()

    with jax.named_scope("forward"):
        from_down, from_up, opposite = down * NC + c, up * NC + c, across * NC + c
        for slot, part, to in ((from_down, 0, up), (from_up, 1, down)):
            w_copy(slot, part).wait_recv()
            v_copy(to, slot, part).start()
            w_copy(slot, part).start()
        send_chunk(1)
        pl.semaphore_wait(greet_a, 2)
        greet(greet_b, 6)
        for slot, part in ((from_down, 1), (from_up, 0), (opposite, 0), (opposite, 1)):
            w_copy(slot, part).wait_recv()
            w_copy(slot, part).start()
        for v in range(NY):
            for part in range(2):
                w_copy(v * NC + 1 - c, part).wait_recv()

    def first_of(half):
        return (pair, cross_of(pair)) if half == 0 else (cross, pair_of(cross))

    def second_of(half):
        return cross if half == 0 else pair

    def block(b):
        return pl.ds(pl.multiple_of(b * 128, 128), 128)

    def x1_copies(j, half):
        to, other = first_of(half)
        return [
            remote(r_buf.at[j, half, block(b)], x1.at[j, half, k], x1_send.at[j, half], x1_recv.at[j, half, k], at(px=to))
            for k, b in ((1, other), (0, to))
        ]

    def x2_copy(j, half):
        return remote(s1.at[j, half], x2.at[j, half], x2_send.at[j, half], x2_recv.at[j, half], at(px=second_of(half)))

    def near_copy(j, v):
        return remote(near_out.at[j, v], near_in.at[j, zl], n_send.at[j], n_recv.at[j], at(pz=zh * 4 + v))

    def far_copy(j, v):
        return remote(far_out.at[j, v], far_in.at[j, zh], f_send.at[j], f_recv.at[j], at(pz=v * 4 + zl))

    def z_copy(j, half, v):
        k, part = j - STEPS, pl.ds(half * 8, 8)
        return remote(z_out.at[k, v, part], z_in.at[k, z, part], z_send.at[k], z_recv.at[k], at(pz=v))

    def stage_mul(j):
        with jax.named_scope("mul"):
            pltpu.make_async_copy(a_buf.at[j], a_buf.at[j], a_recv.at[j]).wait()
            if j + 2 < CH:
                send_chunk(j + 2)
            for half in range(2):
                for v in range(NY):
                    res = jnp.dot(vt[v * NC + half], a_buf[j], preferred_element_type=jnp.float32)
                    for e in range(2):
                        r_buf[j, half, pl.ds(v * 2 + e, 64, stride=8), :] = res[e * 64 : (e + 1) * 64]
                for copy in x1_copies(j, half):
                    copy.start()

    def stage_x1(j):
        with jax.named_scope("x1"):
            for half in range(2):
                copies = x1_copies(j, half)
                copies[0].wait_recv()
                s1[j, half] = r_buf[j, half, block(second_of(half))] + x1[j, half, 1]
                x2_copy(j, half).start()
            for half in range(2):
                x1_copies(j, half)[1].wait_recv()

    def stage_x2(j):
        with jax.named_scope("x2"):
            for half in range(2):
                x2_copy(j, half).wait_recv()
                total = r_buf[j, half, block(x)] + x1[j, half, 0] + x2[j, half]
                for v in range(4):
                    if j < STEPS:
                        near_out[j, v, half * 32 : half * 32 + 32] = total[v * 32 : v * 32 + 32]
                    else:
                        for w in range(4):
                            z_out[j - STEPS, w * 4 + v, half * 8 : half * 8 + 8] = total[v * 32 + w * 8 : v * 32 + w * 8 + 8]
                if j >= STEPS:
                    for v in z_others:
                        z_copy(j, half, v).start()
            if j < STEPS:
                for v in zl_others:
                    near_copy(j, v).start()
                near_in[j, zl] = near_out[j, zl]
            else:
                z_in[j - STEPS, z] = z_out[j - STEPS, z]

    def stage_near(j):
        with jax.named_scope("near"):
            pltpu.make_async_copy(near_in.at[j, pl.ds(0, 3)], near_in.at[j, pl.ds(0, 3)], n_recv.at[j]).wait()
            total = near_in[j, 0] + near_in[j, 1] + near_in[j, 2] + near_in[j, 3]
            for v in range(4):
                for half in range(2):
                    far_out[j, v, half * 8 : half * 8 + 8] = total[half * 32 + v * 8 : half * 32 + v * 8 + 8]
            for v in zh_others:
                far_copy(j, v).start()
            far_in[j, zh] = far_out[j, zh]

    def stage_far(j):
        with jax.named_scope("far"):
            pltpu.make_async_copy(far_in.at[j, pl.ds(0, 3)], far_in.at[j, pl.ds(0, 3)], f_recv.at[j]).wait()
            total = far_in[j, 0] + far_in[j, 1] + far_in[j, 2] + far_in[j, 3]
            keep(j, total)

    def stage_z(j):
        with jax.named_scope("z"):
            got = z_in.at[j - STEPS, pl.ds(0, NZ - 1)]
            pltpu.make_async_copy(got, got, z_recv.at[j - STEPS]).wait()
            keep(j, functools.reduce(jnp.add, [z_in[j - STEPS, v] for v in range(NZ)]))

    def keep(j, total):
        for half in range(2):
            g_buf[pl.ds(half * 64 + j, 8, stride=8), :] = total[half * 8 : half * 8 + 8]

    def bias_stage(k):
        if k == 0:

            @pl.when(x == 0)
            def _():
                pltpu.make_async_copy(bias_x.at[pl.ds(1, 3)], bias_x.at[pl.ds(1, 3)], b_recv.at[0]).wait()
                bias_out[1] = bias_out[0] + bias_x[1] + bias_x[2] + bias_x[3]

                @pl.when(zl != 0)
                def _():
                    remote(bias_out.at[1], bias_n.at[zl], b_send.at[1], b_recv.at[1], at(pz=zh * 4)).start()

        elif k == 1:

            @pl.when((x == 0) & (zl == 0))
            def _():
                pltpu.make_async_copy(bias_n.at[pl.ds(1, 3)], bias_n.at[pl.ds(1, 3)], b_recv.at[1]).wait()
                bias_out[2] = bias_out[1] + bias_n[1] + bias_n[2] + bias_n[3]

                @pl.when(zh != 0)
                def _():
                    remote(bias_out.at[2], bias_f.at[zh], b_send.at[2], b_recv.at[2], at(pz=0)).start()

        else:

            @pl.when(dp == 0)
            def _():
                pltpu.make_async_copy(bias_f.at[pl.ds(1, 3)], bias_f.at[pl.ds(1, 3)], b_recv.at[2]).wait()
                rows[0:8] = bias_out[2] + bias_f[1] + bias_f[2] + bias_f[3]

    rows[0:8] = jnp.zeros((8, LANES), jnp.float32)
    lags = [(stage_mul, 0), (stage_x1, 1), (stage_x2, 2), (stage_near, 3)]
    for step in range(CH + 3):
        if step == CH + 1:
            lags = [lags[3], lags[2]]
        for stage, lag in lags:
            if 0 <= step - lag < (STEPS if stage is stage_near else CH):
                stage(step - lag)
        if step in (1, 3):
            bias_stage(step // 2)
        if step == 2:
            pl.semaphore_wait(greet_b, 2)
    bias_stage(2)
    with jax.named_scope("sent"):
        for part in range(2):
            v_copy(up, mp, part).wait_send()
            v_copy(down, mp, part).wait_send()
        v_copy(up, from_down, 0).wait_send()
        v_copy(down, from_up, 1).wait_send()
        for v in range(NY):
            for part in range(2):
                w_copy(v * NC + c, part).wait_send()
        for j in range(CH):
            for m in mp_others:
                a_copy(j, m).wait_send()
            for half in range(2):
                for copy in x1_copies(j, half):
                    copy.wait_send()
                x2_copy(j, half).wait_send()
    for j in range(STEPS):
        stage_far(j)
    for j in range(STEPS, CH):
        stage_z(j)

    def g_copy(k, m):
        src = g_buf.at[pl.ds(pl.multiple_of(((m % NC) * NY + m // NC) * 16, 16), 16)]
        dst = g_in.at[k, pl.ds(pl.multiple_of(mp * 16, 16), 16)]
        return remote(src, dst, g_send, g_recv.at[k], at(p=dp if k == 0 else before, m=m))

    with jax.named_scope("heads"):
        for m in mp_others + [mp]:
            g_copy(1, m).start()
        for m in mp_others:
            g_copy(0, m).start()
        own = pl.ds(pl.multiple_of(mp * 16, 16), 16)
        g_in[0, own] = g_buf[pl.ds(pl.multiple_of((c * NY + y) * 16, 16), 16)]
        pltpu.make_async_copy(g_in.at[0, pl.ds(0, 112)], g_in.at[0, pl.ds(0, 112)], g_recv.at[0]).wait()
        pltpu.make_async_copy(g_in.at[1], g_in.at[1], g_recv.at[1]).wait()

    with jax.named_scope("update"):
        load[1].wait()
        load[2].wait()
        for k in range(2):
            for m in range(NMP):
                for e in range(2):
                    start = 8 + k * 80 + e * 40 + CH * m
                    rows[start : start + CH] = g_in[k, m * 16 + e * 8 : m * 16 + e * 8 + CH]
        head_total = jnp.sum(rows[0:8] * rows[0:8]) / 8.0
        head_moment = beta_two * block_ref[NMP * HEAD + mp] + (1.0 - beta_two) * (head_total / HEAD)
        denom[0:8] = jnp.full((8, LANES), head_moment, jnp.float32)
        for k in range(4):
            unit = rows[8 + k * 40 : 48 + k * 40]
            unit_moment = beta_two * block_ref[mp * HEAD + 2 * dp + k] + (1.0 - beta_two) * (
                jnp.sum(unit * unit) / WIDTH
            )
            denom[8 + k * 40 : 48 + k * 40] = jnp.full((40, LANES), unit_moment, jnp.float32)
        grad = rows[pl.ds(dp + 7, ROWS_P), :]
        moment = denom[pl.ds(dp + 7, ROWS_P), :]
        momentum = beta_one * first_ref[...] + (1.0 - beta_one) * grad
        step_dir = momentum / bias_one / (jnp.sqrt(moment / bias_two) + epsilon)
        position = dp * ROWS_P + lax.broadcasted_iota(jnp.int32, (ROWS_P, LANES), 0)
        out_ref[...] = jnp.where(position < USED_ROWS, step_dir, 0.0)
        store = pltpu.make_async_copy(out_ref, out_hbm.at[:, 0], in_sem.at[3])
        store.start()

    with jax.named_scope("drain"):
        store.wait()
        for j in range(STEPS):
            for v in zl_others:
                near_copy(j, v).wait_send()
            for v in zh_others:
                far_copy(j, v).wait_send()
        for j in range(STEPS, CH):
            for v in z_others:
                for half in range(2):
                    z_copy(j, half, v).wait_send()
        for m in mp_others:
            g_copy(0, m).wait_send()
        for m in range(NMP):
            g_copy(1, m).wait_send()

        @pl.when(x != 0)
        def _():
            remote(bias_out.at[0], bias_x.at[x], b_send.at[0], b_recv.at[0], at(px=0)).wait_send()

        @pl.when((x == 0) & (zl != 0))
        def _():
            remote(bias_out.at[1], bias_n.at[zl], b_send.at[1], b_recv.at[1], at(pz=zh * 4)).wait_send()

        @pl.when((x == 0) & (zl == 0) & (zh != 0))
        def _():
            remote(bias_out.at[2], bias_f.at[zh], b_send.at[2], b_recv.at[2], at(pz=0)).wait_send()


def body(value_grads, activations, block_moment, first_moment):
    f32, bf16 = jnp.float32, jnp.bfloat16
    dma = pltpu.SemaphoreType.DMA
    update = pl.pallas_call(
        kernel,
        out_shape=jax.ShapeDtypeStruct((ROWS_P, 1, LANES), f32),
        in_specs=[pl.BlockSpec(memory_space=pltpu.HBM)] * 4,
        out_specs=pl.BlockSpec(memory_space=pltpu.HBM),
        scratch_shapes=[
            pltpu.VMEM(value_grads.shape, bf16),
            pltpu.SMEM(block_moment.shape, f32),
            pltpu.VMEM((ROWS_P, LANES), f32),
            pltpu.VMEM((ROWS_P, LANES), f32),
            pltpu.VMEM((CH, NMP, TOK, LANES), bf16),
            pltpu.VMEM((NMP, HEAD, TOKENS), bf16),
            pltpu.VMEM((CH, TOKENS, LANES), bf16),
            pltpu.VMEM((CH, 2, 512, LANES), f32),
            pltpu.VMEM((CH, 2, 2, 128, LANES), f32),
            pltpu.VMEM((CH, 2, 128, LANES), f32),
            pltpu.VMEM((CH, 2, 128, LANES), f32),
            pltpu.VMEM((CH, 4, 64, LANES), f32),
            pltpu.VMEM((CH, 4, 64, LANES), f32),
            pltpu.VMEM((CH, 4, 16, LANES), f32),
            pltpu.VMEM((CH, 4, 16, LANES), f32),
            pltpu.VMEM((128, LANES), f32),
            pltpu.VMEM((2, 128, LANES), f32),
            pltpu.VMEM((168, LANES), f32),
            pltpu.VMEM((168, LANES), f32),
            pltpu.VMEM((3, 8, LANES), f32),
            pltpu.VMEM((4, 8, LANES), f32),
            pltpu.VMEM((4, 8, LANES), f32),
            pltpu.VMEM((4, 8, LANES), f32),
            pltpu.VMEM((CH - STEPS, NZ, 16, LANES), f32),
            pltpu.VMEM((CH - STEPS, NZ, 16, LANES), f32),
            dma((4,)), dma((CH,)), dma((CH - STEPS,)), dma((CH - STEPS,)),
            pltpu.SemaphoreType.REGULAR, pltpu.SemaphoreType.REGULAR,
            dma, dma((NMP, 2)), dma, dma((CH,)), dma((CH,)),
            dma((CH, 2)), dma((CH, 2, 2)), dma((CH, 2)), dma((CH, 2)),
            dma((CH,)), dma((CH,)), dma((CH,)), dma((CH,)),
            dma, dma((2,)), dma((3,)), dma((3,)),
        ],
        compiler_params=pltpu.CompilerParams(
            collective_id=0, has_side_effects=True, vmem_limit_bytes=63 << 20
        ),
        name="gradient_step",
    )(value_grads, activations, block_moment, first_moment.reshape(ROWS_P, 1, LANES))
    return update.reshape(first_moment.shape)


def solution(mesh):
    return jax.shard_map(
        body,
        mesh=mesh,
        in_specs=(P("dp", "mp"), P(("dp", "mp"), None), P(), P("mp", "dp", None)),
        out_specs=P("mp", "dp", None),
        check_vma=False,
    )
```
